512 devices in a mesh: leaf: 128 (over z, y, core), grp: 4 (over x).
Axes of the slice: x: 4, y: 8, z: 8, core: 2. Of those that a mesh axis runs over, the one named last changes fastest.
Arguments:
- points_in: bfloat16 [64, 262144], P('grp', 'leaf'), may hold values from -6 to 6
- leaf_basis: bfloat16 [32, 262144], P(None, 'leaf'), may hold values from -0.75 to 0.75
- transfer: bfloat16 [4096, 1024], P('leaf'), may hold values from -0.375 to 0.375
- far_blocks: bfloat16 [4096, 16, 1024], P('leaf'), may hold values from -0.25 to 0.25
- near_blocks: bfloat16 [4096, 8, 4096], P('leaf'), may hold values from -0.25 to 0.25
- near_leaf: int32 [4096, 8], P('leaf'), may hold values from 0 to 4095, as said below
- near_count: int32 [4096], P('leaf'), may hold values from 4 to 8, as said below
- far_slots: int32 [4096, 16], P('leaf'), may hold values from 0 to 127, as said below
- far_count: int32 [4096], P('leaf'), may hold values from 8 to 16, as said below
- recv_rows: int32 [128, 128, 1], P('leaf'), may hold values from 0 to 31
- coarse_blocks: bfloat16 [512, 16, 1024], P('leaf', 'grp'), may hold values from -0.25 to 0.25
- coarse_far: int32 [512, 16], P('leaf'), may hold values from 0 to 511, as said below
- coarse_count: int32 [512], P('leaf'), may hold values from 8 to 16, as said below
Outputs:
- field_out: bfloat16 [64, 262144], P('grp', 'leaf')
The draws below stay inside these ranges and needn't reach their ends.
Inputs may be any that keep to these rules, and one draw needn't show every extreme that they name: near_leaf[l, 0] = l, and every entry lies within 4 leaves of l. `near_count`: some leaf has all 8 entries live. `far_slots`: entries index a device's requested slots flattened as owning device times 1 plus slot. `far_count`: some leaf has all 16 entries live. `coarse_far`: entries of coarse node c name coarse nodes held by the same aligned group of 16 indices of leaf as c. `coarse_count`: some coarse node has all 16 entries live.
All inputs are finite; a program needn't handle non-finite values.
Results may differ from the reference program's by a relative error of at most 0.0044.
Values may be sent and summed in bfloat16 or wider, within the bound.
A program may use at most 64 MiB of HBM per device.

```python
import jax
import jax.numpy as jnp
from jax import lax

RHS = 64
PTS = 64
RANK = 32
CHILD = 8
K_NEAR = 8
K_FAR = 16
K_CFAR = 16
WIN = 4
LEAF_DEV = 32
GROUP = 16
LEAVES = 4096
COARSE = 512
SLOTS = 1
NPTS = 262144
N_LEAF = 128


def forced_counts(key, length, top):
    first, second, third = jax.random.split(key, 3)
    counts = jax.random.randint(first, (length,), top // 2, top + 1)
    spot_high = jax.random.randint(second, (), 0, length)
    spot_low = jax.random.randint(third, (), 0, length)
    where_index = jnp.arange(length)
    counts = jnp.where(where_index == spot_low, top // 2, counts)
    counts = jnp.where(where_index == spot_high, top, counts)
    return counts.astype(jnp.int32)


def draw_near_leaf(key, part):
    key = jax.random.fold_in(key, 11)
    offsets = jax.random.randint(key, (LEAVES, K_NEAR), -WIN, WIN + 1)
    column = jnp.arange(K_NEAR)[None, :]
    offsets = jnp.where(column == 0, 0, offsets)
    rows = jnp.arange(LEAVES)[:, None] + offsets
    return jnp.clip(rows, 0, LEAVES - 1).astype(jnp.int32)


def draw_near_count(key, part):
    key = jax.random.fold_in(key, 12)
    return forced_counts(key, LEAVES, K_NEAR)


def draw_far_slots(key, part):
    key = jax.random.fold_in(key, 13)
    first, second = jax.random.split(key)
    total = N_LEAF * SLOTS
    entries = LEAF_DEV * K_FAR
    keys = jax.random.split(first, N_LEAF)
    base = jax.vmap(lambda single: jax.random.permutation(single, total))(keys)
    extra = jax.random.randint(second, (N_LEAF, entries), 0, total)
    position = jnp.arange(entries)
    picked = base[:, jnp.minimum(position, total - 1)]
    values = jnp.where(position[None, :] < total, picked, extra)
    values = values.reshape(N_LEAF, K_FAR, LEAF_DEV).transpose(0, 2, 1)
    return values.reshape(LEAVES, K_FAR).astype(jnp.int32)


def draw_far_count(key, part):
    key = jax.random.fold_in(key, 14)
    return forced_counts(key, LEAVES, K_FAR)


def draw_coarse_far(key, part):
    key = jax.random.fold_in(key, 16)
    per_group = GROUP * (LEAF_DEV // CHILD)
    offsets = jax.random.randint(key, (COARSE, K_CFAR), 0, per_group)
    starts = jnp.arange(COARSE) // per_group * per_group
    return (starts[:, None] + offsets).astype(jnp.int32)


def draw_coarse_count(key, part):
    key = jax.random.fold_in(key, 15)
    return forced_counts(key, COARSE, K_CFAR)


def touch_ends(values, rng, least, high):
    longest = values.shape.index(max(values.shape))
    spots = []
    for shift in (0, 1):
        where = [jax.random.randint(jax.random.fold_in(rng, axis), (), 0, length) for axis, length in enumerate(values.shape)]
        where[longest] = (where[longest] + shift) % values.shape[longest]
        spots.append(tuple(where))
    return values.at[spots[0]].set(least).at[spots[1]].set(high)


def level_of(key, extent, cuts, low, high):
    factor_of = 1.0
    for axis_at, shards_of in cuts:
        draws = jax.random.uniform(jax.random.fold_in(jax.random.fold_in(key, 6), axis_at), (shards_of,), jnp.float32, low / len(cuts), high / len(cuts))
        factor_of = factor_of * jnp.repeat(jnp.exp(draws), extent[axis_at] // shards_of).reshape((-1,) + (1,) * (len(extent) - 1 - axis_at))
    return factor_of


def bell_draw(rng, extent, deviation, most, shards=(), kind=jnp.bfloat16):
    loudness = level_of(rng, extent, shards, -0.22, 0.18) if shards else 1.0
    values = jax.random.normal(rng, extent, jnp.float32) * deviation * loudness
    return jnp.minimum(jnp.maximum(values, -most), most).astype(kind)


def setup_inputs(seed: int = 0) -> dict:
    seeds = jax.random.split(jax.random.key(seed), 14)
    points_in = bell_draw(seeds[0], (RHS, NPTS), 1.0, 6.0, ((0, 4), (1, 128)))
    leaf_basis = bell_draw(seeds[1], (RANK, NPTS), PTS ** -0.5, 0.75, ((1, 128),))
    transfer = bell_draw(seeds[2], (LEAVES, RANK * RANK), (RANK * CHILD) ** -0.5, 0.375, ((0, 128),))
    far_blocks = bell_draw(seeds[3], (LEAVES, K_FAR, RANK * RANK), (RANK * K_FAR) ** -0.5, 0.25, ((0, 128),))
    near_blocks = bell_draw(seeds[4], (LEAVES, K_NEAR, PTS * PTS), (PTS * K_NEAR) ** -0.5, 0.25, ((0, 128),))
    near_leaf = draw_near_leaf(jax.random.fold_in(seeds[13], 71), 0)
    near_count = draw_near_count(jax.random.fold_in(seeds[13], 71), 0)
    far_slots = draw_far_slots(jax.random.fold_in(seeds[13], 71), 0)
    far_count = draw_far_count(jax.random.fold_in(seeds[13], 71), 0)
    recv_rows = touch_ends(jax.random.randint(seeds[9], (N_LEAF, N_LEAF, SLOTS), 0, LEAF_DEV), jax.random.fold_in(seeds[9], 1), 0, LEAF_DEV - 1).astype(jnp.int32)
    coarse_blocks = bell_draw(seeds[10], (COARSE, K_CFAR, RANK * RANK), (RANK * K_CFAR) ** -0.5, 0.25, ((0, 128), (1, 4)))
    coarse_far = draw_coarse_far(jax.random.fold_in(seeds[13], 71), 0)
    coarse_count = draw_coarse_count(jax.random.fold_in(seeds[13], 71), 0)
    return dict(points_in=points_in, leaf_basis=leaf_basis, transfer=transfer, far_blocks=far_blocks, near_blocks=near_blocks, near_leaf=near_leaf, near_count=near_count, far_slots=far_slots, far_count=far_count, recv_rows=recv_rows, coarse_blocks=coarse_blocks, coarse_far=coarse_far, coarse_count=coarse_count)


def live_mask(counts, entries):
    return (jnp.arange(entries)[None, :] < counts[:, None]).astype(jnp.float32)


def reference(points_in, leaf_basis, transfer, far_blocks, near_blocks, near_leaf, near_count, far_slots, far_count, recv_rows, coarse_blocks, coarse_far, coarse_count):
    points_f = points_in.reshape(RHS, LEAVES, PTS).astype(jnp.float32)
    basis_f = leaf_basis.reshape(RANK, LEAVES, PTS).astype(jnp.float32)
    coef = jnp.einsum('rlp,qlp->lrq', basis_f, points_f).astype(jnp.bfloat16)
    maps = transfer.reshape(LEAVES, RANK, RANK).astype(jnp.float32)
    lifted = jnp.einsum('lrs,lsq->lrq', maps, coef.astype(jnp.float32))
    parent = lifted.reshape(COARSE, CHILD, RANK, RHS).sum(axis=1).astype(jnp.bfloat16)
    cmask = live_mask(coarse_count, K_CFAR)
    cblocks = coarse_blocks.reshape(COARSE, K_CFAR, RANK, RANK).astype(jnp.float32) * cmask[:, :, None, None]
    csource = parent[coarse_far].astype(jnp.float32)
    coarse_field = jnp.einsum('ckrs,cksq->crq', cblocks, csource).astype(jnp.bfloat16)
    down = jnp.einsum('lrs,lrq->lsq', maps, jnp.repeat(coarse_field.astype(jnp.float32), CHILD, axis=0))
    table = recv_rows.reshape(N_LEAF, N_LEAF * SLOTS)
    owner = (jnp.arange(LEAVES) // LEAF_DEV).astype(jnp.int32)
    source = ((far_slots // SLOTS) * LEAF_DEV + table[owner[:, None], far_slots]).astype(jnp.int32)
    fmask = live_mask(far_count, K_FAR)

    def far_block(items):
        blocks, indices, masks = items
        gathered = coef[indices].astype(jnp.float32)
        weights = blocks.reshape(LEAF_DEV, K_FAR, RANK, RANK).astype(jnp.float32) * masks[:, :, None, None]
        return jnp.einsum('lkrs,lksq->lrq', weights, gathered)

    far_part = lax.map(far_block, (far_blocks.reshape(N_LEAF, LEAF_DEV, K_FAR, RANK * RANK), source.reshape(N_LEAF, LEAF_DEV, K_FAR), fmask.reshape(N_LEAF, LEAF_DEV, K_FAR)))
    far_part = far_part.reshape(LEAVES, RANK, RHS)
    local = (far_part + down).astype(jnp.bfloat16)
    points_t = points_in.reshape(RHS, LEAVES, PTS).transpose(1, 0, 2)
    nmask = live_mask(near_count, K_NEAR)

    def near_block(items):
        blocks, indices, masks = items
        gathered = points_t[indices].astype(jnp.float32)
        weights = blocks.reshape(LEAF_DEV, K_NEAR, PTS, PTS).astype(jnp.float32) * masks[:, :, None, None]
        return jnp.einsum('lkps,lkqs->qlp', weights, gathered)

    near = lax.map(near_block, (near_blocks.reshape(N_LEAF, LEAF_DEV, K_NEAR, PTS * PTS), near_leaf.reshape(N_LEAF, LEAF_DEV, K_NEAR), nmask.reshape(N_LEAF, LEAF_DEV, K_NEAR)))
    near = near.transpose(1, 0, 2, 3).reshape(RHS, LEAVES, PTS)
    result = jnp.einsum('rlp,lrq->qlp', basis_f, local.astype(jnp.float32)) + near
    return result.reshape(RHS, NPTS).astype(jnp.bfloat16)
```

```python
import jax
import jax.numpy as jnp
from jax import lax
from jax.experimental import pallas as pl
from jax.experimental.pallas import tpu as pltpu
from jax.sharding import PartitionSpec as P

BF = jnp.bfloat16
F32 = jnp.float32
MESH = pl.DeviceIdType.MESH


def dot_nt(a, b):
    return lax.dot_general(a, b, (((1,), (1,)), ((), ())), preferred_element_type=F32)


def dot_nn(a, b):
    return jnp.dot(a, b, preferred_element_type=F32)


def iotas(shape):
    row = lax.broadcasted_iota(jnp.int32, shape, 0)
    col = lax.broadcasted_iota(jnp.int32, shape, 1)
    return row, col


def ones_where(cond):
    return jnp.where(cond, 1.0, 0.0).astype(BF)


def expand(tiles):
    _, col = iotas((8, 128))
    masks = [jnp.where((col >> 5) == r4, 1.0, 0.0) for r4 in range(4)]
    return jnp.concatenate([tile * mask for tile in tiles for mask in masks], axis=0).astype(BF)


def lane_tiles(value):
    return [value[:, 128 * t : 128 * t + 128] for t in range(value.shape[1] // 128)]


def diagonal(product, rows, entries):
    _, col = iotas((rows, product.shape[1]))
    kept = product[0:rows]
    for k in range(1, entries):
        kept = jnp.where((col & (entries - 1)) == k, product[rows * k : rows * k + rows], kept)
    return kept


def spread_matrix():
    row, col = iotas((128, 512))
    return ones_where(((row >> 5) == (col >> 7)) & ((row & 31) == (col & 31)))


def place_matrix(j):
    row, col = iotas((128, 512))
    return ones_where(((row >> 5) == (col >> 7)) & ((col & 127) == (j * 32 + (row & 31))))


def kernel(
    points_h,
    basis_h,
    transfer_h,
    far_h,
    near_h,
    near_leaf_h,
    near_count_h,
    far_slots_h,
    far_count_h,
    recv_h,
    coarse_h,
    coarse_far_h,
    coarse_count_h,
    out_ref,
    pts,
    bas,
    trn,
    farv,
    nearv,
    cb,
    halo,
    p1,
    rown,
    pw,
    tp,
    r2,
    send,
    fbuf,
    tt,
    bx,
    tn,
    nr,
    nf,
    fr,
    dr,
    idxv,
    idxs,
    nls,
    ncs,
    fss,
    fcs,
    cfs,
    ccs,
    load_sem,
    idx_ssem,
    idx_rsem,
    p1_ssem,
    p1_rsem,
    p2_ssem,
    p2_rsem,
    pw_ssem,
    pw_rsem,
    halo_ssem,
    halo_rsem,
    cb_ssem,
    cb_rsem,
):
    me = lax.axis_index("leaf")
    grp = lax.axis_index("grp")
    core = lax.rem(me, 2)
    ylo = lax.rem(lax.div(me, 2), 2)
    yhi = lax.rem(lax.div(me, 4), 4)
    zlo = lax.rem(lax.div(me, 16), 2)
    zhi = lax.div(me, 32)
    member = zlo * 4 + ylo * 2 + core
    in_group = lax.rem(me, 16)

    def cube_peer(o):
        c = lax.rem(core + (o & 1), 2)
        y = lax.rem(ylo + ((o >> 1) & 1), 2)
        z = lax.rem(zlo + ((o >> 2) & 1), 2)
        return (zhi * 32 + z * 16 + yhi * 4 + y * 2 + c, grp)

    def far_peer(o):
        z = lax.rem(zhi + (o >> 2), 4)
        y = lax.rem(yhi + (o & 3), 4)
        return (z * 32 + zlo * 16 + y * 4 + ylo * 2 + core, grp)

    def group_peer(o):
        return (lax.div(me, 16) * 16 + lax.rem(in_group + o, 16), grp)

    up = (lax.rem(me + 1, 128), grp)
    down = (lax.rem(me + 127, 128), grp)

    def grp_peer(o):
        return (me, lax.rem(grp + o, 4))

    loads = {}

    def load(name, src, dst, n):
        loads[name] = pltpu.make_async_copy(src, dst, load_sem.at[n])
        loads[name].start()

    load("points", points_h, pts, 0)
    load("basis", basis_h, bas, 1)
    load("transfer", transfer_h, trn, 2)
    load("recv", recv_h, idxv.at[0], 3)
    load("coarse", coarse_h, cb.at[grp], 4)

    barrier = pltpu.get_barrier_semaphore()
    peers = [cube_peer(o) for o in range(1, 8)]
    peers += [far_peer(o) for o in range(1, 16)]
    peers += [group_peer(o) for o in range(1, 16)]
    peers += [up, down]
    peers += [grp_peer(o) for o in range(1, 4)]
    for peer in peers:
        pl.semaphore_signal(barrier, inc=1, device_id=peer, device_id_type=MESH)

    load("near_leaf", near_leaf_h, nls, 5)
    load("near_count", near_count_h, ncs, 6)
    load("far_slots", far_slots_h, fss, 7)
    load("far_count", far_count_h, fcs, 8)
    load("coarse_far", coarse_far_h, cfs, 9)
    load("coarse_count", coarse_count_h, ccs, 10)
    load("near", near_h, nearv, 11)
    load("far", far_h, farv, 12)

    loads["points"].wait()
    loads["basis"].wait()
    _, col = iotas((32, 256))
    quad_masks = [ones_where((col >> 6) == l4) for l4 in range(4)]
    for quad in range(8):
        lanes = slice(256 * quad, 256 * quad + 256)
        v = bas[:, lanes]
        vv = jnp.concatenate([v * mask for mask in quad_masks], axis=0)
        p1[member, quad] = dot_nt(pts[:, lanes], vv).astype(BF)

    spread = spread_matrix()
    wide = dot_nn(p1[member].reshape(128, 128), spread).astype(BF)
    for quad in range(8):
        for a in range(4):
            rown[4 * quad + a] = wide[16 * quad : 16 * quad + 16, 128 * a : 128 * a + 128]
    loads["transfer"].wait()
    total = jnp.zeros((16, 128), F32)
    row, col = iotas((256, 128))
    for c in range(4):
        ex = expand(lane_tiles(trn[8 * c : 8 * c + 8, :].astype(F32)))
        product = dot_nt(rown[8 * c : 8 * c + 8].reshape(128, 128), ex)
        kept = diagonal(product, 16, 8).astype(BF)
        total += dot_nn(kept, ones_where(col == c * 32 + (row >> 3)))
    pw[in_group] = total.astype(BF)

    loads["recv"].wait()
    loads["coarse"].wait()
    pl.semaphore_wait(barrier, len(peers))

    sends = []

    def remote(src, dst, ssem, rsem, peer):
        copy = pltpu.make_async_remote_copy(
            src_ref=src,
            dst_ref=dst,
            send_sem=ssem,
            recv_sem=rsem,
            device_id=peer,
            device_id_type=MESH,
        )
        copy.start()
        sends.append(copy)
        return copy

    p1_copies = [
        remote(p1.at[member], p1.at[member], p1_ssem.at[o], p1_rsem.at[o], cube_peer(o))
        for o in range(1, 8)
    ]
    idx_copies = [
        remote(idxv.at[0], idxv.at[o], idx_ssem.at[o], idx_rsem.at[o], far_peer(o))
        for o in range(1, 16)
    ]
    halo_copies = [
        remote(pts.at[:, pl.ds(1792, 256)], halo.at[0], halo_ssem.at[0], halo_rsem.at[0], up),
        remote(pts.at[:, pl.ds(0, 256)], halo.at[1], halo_ssem.at[1], halo_rsem.at[1], down),
    ]
    pw_copies = [
        remote(pw.at[in_group], pw.at[in_group], pw_ssem.at[o], pw_rsem.at[o], group_peer(o))
        for o in range(1, 16)
    ]
    cb_copies = [
        remote(cb.at[grp], cb.at[grp], cb_ssem.at[o], cb_rsem.at[o], grp_peer(o))
        for o in range(1, 4)
    ]

    loads["far"].wait()
    loads["far_count"].wait()

    def prepare(l, _):
        count = fcs[0, l]
        sub, _ = iotas((8, 128))
        low = jnp.where(sub < count, 1.0, 0.0)
        high = jnp.where(sub + 8 < count, 1.0, 0.0)
        blocks = farv[l].astype(F32)
        bx[l, :, 0:128] = expand([tile * low for tile in lane_tiles(blocks[0:8])])
        bx[l, :, 128:256] = expand([tile * high for tile in lane_tiles(blocks[8:16])])
        return 0

    lax.fori_loop(0, 32, prepare, 0)

    _, col = iotas((16, 128))
    left = jnp.where(col < 64, 1.0, 0.0)
    right = 1.0 - left

    def near_table(m, tile):
        value = tile.astype(F32)
        turned = pltpu.roll(value, 64, 1)
        tn[m] = jnp.concatenate([value * left, turned * right], axis=0).astype(BF)
        tn[m + 1] = jnp.concatenate([turned * left, value * right], axis=0).astype(BF)

    for j in range(16):
        near_table(4 + 2 * j, pts[:, 128 * j : 128 * j + 128])
    for copy in halo_copies:
        copy.wait_recv()
    for j in range(2):
        near_table(2 * j, halo[0, :, 128 * j : 128 * j + 128])
        near_table(36 + 2 * j, halo[1, :, 128 * j : 128 * j + 128])
    loads["near"].wait()
    loads["near_leaf"].wait()
    loads["near_count"].wait()

    def near_pair(j, _):
        _, lane = iotas((32, 256))
        for l2 in range(2):
            l = 2 * j + l2
            blocks = nearv[l].astype(F32)
            flat = jnp.concatenate(lane_tiles(blocks), axis=0).astype(BF)
            source = jnp.concatenate(
                [tn[jnp.clip(nls[k, l] - me * 32 + 4, 0, 39)] for k in range(8)], axis=0
            )
            kept = diagonal(dot_nt(source, flat), 32, 8)
            kept = jnp.where((lane & 7) < ncs[0, l], kept, 0.0).astype(BF)
            nr[j, :, 512 * l2 : 512 * l2 + 256] = kept[0:16]
            nr[j, :, 512 * l2 + 256 : 512 * l2 + 512] = kept[16:32]
        return 0

    lax.fori_loop(0, 8, near_pair, 0)

    for copy in p1_copies:
        copy.wait_recv()
    for copy in idx_copies:
        copy.wait_recv()
    to_smem = pltpu.make_async_copy(idxv, idxs, load_sem.at[13])
    to_smem.start()
    for j in range(4):
        place = place_matrix(j)
        for zl in range(2):
            m = 4 * zl + j
            wide = dot_nn(p1[m].reshape(128, 128), place).astype(BF)
            for quad in range(8):
                for a in range(4):
                    r2[32 * m + 4 * quad + a] = wide[
                        16 * quad : 16 * quad + 16, 128 * a : 128 * a + 128
                    ]
    to_smem.wait()
    p2_copies = []
    for o in list(range(1, 16)) + [0]:
        slot = ((4 - (o >> 2)) % 4) * 4 + (4 - (o & 3)) % 4
        for zl in range(2):
            first = zhi * 32 + zl * 16 + yhi * 4
            tile = r2[32 * (4 * zl) + idxs[slot, 0, first]]
            for j in range(1, 4):
                tile = tile + r2[32 * (4 * zl + j) + idxs[slot, 0, first + j]]
            if o == 0:
                fbuf[zhi, zl, yhi] = tile
            else:
                send[o, zl] = tile
        if o:
            p2_copies.append(
                remote(
                    send.at[o],
                    fbuf.at[zhi, :, yhi],
                    p2_ssem.at[o],
                    p2_rsem.at[o],
                    far_peer(o),
                )
            )

    lax.fori_loop(8, 16, near_pair, 0)
    row, col = iotas((1024, 128))
    group = row >> 8
    fold_near = ones_where(col == (group >> 1) * 64 + ((row & 255) >> 3) * 2 + (group & 1))
    nf[...] = dot_nn(nr[...].reshape(256, 1024), fold_near)

    for copy in pw_copies:
        copy.wait_recv()
    wide = dot_nn(pw[...].reshape(256, 128), spread).astype(BF)
    for device in range(16):
        for c in range(4):
            tp[4 * device + c] = wide[16 * device : 16 * device + 16, 128 * c : 128 * c + 128]
    for copy in cb_copies:
        copy.wait_recv()
    loads["coarse_far"].wait()
    loads["coarse_count"].wait()
    total = jnp.zeros((16, 128), F32)
    sub, _ = iotas((8, 1024))
    row, col = iotas((256, 128))
    for cp in range(2):
        counts = jnp.where(sub < 4, ccs[0, 2 * cp], ccs[0, 2 * cp + 1])
        product = jnp.zeros((128, 256), F32)
        for gp in range(2):
            halves = []
            for g in (2 * gp, 2 * gp + 1):
                rows = jnp.concatenate(
                    [cb[g, 2 * cp].astype(F32), cb[g, 2 * cp + 1].astype(F32)], axis=0
                )
                rows = jnp.where((sub & 3) + 4 * g < counts, rows, 0.0)
                halves.append(expand(lane_tiles(rows)))
            weights = jnp.concatenate(halves, axis=1)
            source = jnp.concatenate(
                [
                    jnp.concatenate(
                        [
                            tp[cfs[2 * cp + (k >> 2), 4 * g + (k & 3)] & 63]
                            for g in (2 * gp, 2 * gp + 1)
                        ],
                        axis=1,
                    )
                    for k in range(8)
                ],
                axis=0,
            )
            product += dot_nt(source, weights)
        kept = diagonal(product, 16, 8).astype(BF)
        target = (2 * cp + ((row & 7) >> 2)) * 32 + (row >> 3)
        total += dot_nn(kept, ones_where(col == target))
    field = total.astype(BF)

    row, col = iotas((128, 256))
    flat = jnp.concatenate(lane_tiles(trn[...]), axis=0)
    spreads = []
    for r4 in range(4):
        hit = ((row >> 5) == ((col & 31) >> 3)) & (((row & 31) >> 2) == (col >> 5))
        spreads.append(dot_nn(field, ones_where(hit & ((row & 3) == r4))).astype(BF))
    _, lane = iotas((16, 256))
    _, col = iotas((16, 128))
    for part in range(4):
        pieces = []
        for l in range(8 * part, 8 * part + 8):
            mask = ones_where((lane & 31) == l)
            pieces += [spreads[r4] * mask for r4 in range(4)]
        product = dot_nn(jnp.concatenate(pieces, axis=0), flat)
        for i in range(8):
            kept = product[64 * i : 64 * i + 16]
            for r4 in range(1, 4):
                at = 64 * i + 16 * r4
                kept = jnp.where((col >> 5) == r4, product[at : at + 16], kept)
            dr[8 * part + i] = kept.astype(BF)

    loads["far_slots"].wait()
    for copy in p2_copies:
        copy.wait_recv()
    wide = dot_nn(fbuf[...].reshape(512, 128), spread).astype(BF)
    for quad in range(32):
        for a in range(4):
            tt[4 * quad + a] = wide[16 * quad : 16 * quad + 16, 128 * a : 128 * a + 128]

    def far_part(step, _):
        for i in range(4):
            l = 4 * step + i
            source = jnp.concatenate(
                [
                    jnp.concatenate([tt[fss[k, l]], tt[fss[k + 8, l]]], axis=1)
                    for k in range(8)
                ],
                axis=0,
            )
            fr[l] = diagonal(dot_nt(source, bx[l]), 16, 8).astype(BF)
        return 0

    lax.fori_loop(0, 8, far_part, 0)

    row, col = iotas((256, 32))
    local = dot_nn(fr[...].reshape(512, 256), ones_where(col == (row >> 3)))
    row, col = iotas((128, 32))
    local += dot_nn(dr[...].reshape(512, 128), ones_where(col == (row & 31)))
    local = local.astype(BF)
    _, col = iotas((16, 128))
    for j in range(16):
        both = dot_nn(local[32 * j : 32 * j + 32], bas[:, 128 * j : 128 * j + 128])
        field = jnp.where(col < 64, both[0:16], both[16:32])
        out_ref[:, 128 * j : 128 * j + 128] = (field + nf[16 * j : 16 * j + 16]).astype(BF)

    for copy in sends:
        copy.wait_send()


def per_device(
    points_in,
    leaf_basis,
    transfer,
    far_blocks,
    near_blocks,
    near_leaf,
    near_count,
    far_slots,
    far_count,
    recv_rows,
    coarse_blocks,
    coarse_far,
    coarse_count,
):
    vmem = pltpu.VMEM
    smem = pltpu.SMEM
    dma = pltpu.SemaphoreType.DMA
    anywhere = pl.BlockSpec(memory_space=pltpu.HBM)
    return pl.pallas_call(
        kernel,
        out_shape=jax.ShapeDtypeStruct((16, 2048), BF),
        in_specs=[anywhere] * 13,
        out_specs=pl.BlockSpec(memory_space=pltpu.VMEM),
        scratch_shapes=[
            vmem((16, 2048), BF),
            vmem((32, 2048), BF),
            vmem((32, 1024), BF),
            vmem((32, 16, 1024), BF),
            vmem((32, 8, 4096), BF),
            vmem((4, 4, 4, 1024), BF),
            vmem((2, 16, 256), BF),
            vmem((8, 8, 16, 128), BF),
            vmem((32, 16, 128), BF),
            vmem((16, 16, 128), BF),
            vmem((64, 16, 128), BF),
            vmem((256, 16, 128), BF),
            vmem((16, 2, 16, 128), BF),
            vmem((4, 2, 4, 16, 128), BF),
            vmem((128, 16, 128), BF),
            vmem((32, 256, 256), BF),
            vmem((40, 32, 128), BF),
            vmem((16, 16, 1024), BF),
            vmem((256, 128), F32),
            vmem((32, 16, 256), BF),
            vmem((32, 16, 128), BF),
            vmem((16, 1, 128), jnp.int32),
            smem((16, 1, 128), jnp.int32),
            smem((8, 32), jnp.int32),
            smem((1, 32), jnp.int32),
            smem((16, 32), jnp.int32),
            smem((1, 32), jnp.int32),
            smem((4, 16), jnp.int32),
            smem((1, 4), jnp.int32),
            dma((14,)),
            dma((16,)),
            dma((16,)),
            dma((8,)),
            dma((8,)),
            dma((16,)),
            dma((16,)),
            dma((16,)),
            dma((16,)),
            dma((2,)),
            dma((2,)),
            dma((4,)),
            dma((4,)),
        ],
        compiler_params=pltpu.CompilerParams(
            collective_id=0, has_side_effects=True, vmem_limit_bytes=63 * 1024 * 1024
        ),
        cost_estimate=pl.CostEstimate(
            flops=60_000_000, bytes_accessed=3_600_000, transcendentals=0
        ),
    )(
        points_in,
        leaf_basis,
        transfer,
        far_blocks,
        near_blocks,
        near_leaf.T,
        near_count.reshape(1, 32),
        far_slots.T,
        far_count.reshape(1, 32),
        recv_rows.reshape(1, 128),
        coarse_blocks,
        coarse_far,
        coarse_count.reshape(1, 4),
    )


def solution(mesh):
    in_specs = (
        P("grp", "leaf"),
        P(None, "leaf"),
        P("leaf", None),
        P("leaf", None, None),
        P("leaf", None, None),
        P("leaf", None),
        P("leaf"),
        P("leaf", None),
        P("leaf"),
        P("leaf", None, None),
        P("leaf", "grp", None),
        P("leaf", None),
        P("leaf"),
    )
    out_specs = P("grp", "leaf")
    return jax.shard_map(
        per_device, mesh=mesh, in_specs=in_specs, out_specs=out_specs, check_vma=False
    )
```

```python
import jax
import jax.numpy as jnp
from jax import lax
from jax.experimental import pallas as pl
from jax.experimental.pallas import tpu as pltpu
from jax.sharding import PartitionSpec as P

BF = jnp.bfloat16
F32 = jnp.float32
MESH = pl.DeviceIdType.MESH


def dot_nt(a, b):
    return lax.dot_general(a, b, (((1,), (1,)), ((), ())), preferred_element_type=F32)


def dot_nn(a, b):
    return jnp.dot(a, b, preferred_element_type=F32)


def iotas(shape):
    row = lax.broadcasted_iota(jnp.int32, shape, 0)
    col = lax.broadcasted_iota(jnp.int32, shape, 1)
    return row, col


def ones_where(cond):
    return jnp.where(cond, 1.0, 0.0).astype(BF)


def expand(tiles):
    _, col = iotas((8, 128))
    masks = [jnp.where((col >> 5) == r4, 1.0, 0.0) for r4 in range(4)]
    return jnp.concatenate([tile * mask for tile in tiles for mask in masks], axis=0).astype(BF)


def lane_tiles(value):
    return [value[:, 128 * t : 128 * t + 128] for t in range(value.shape[1] // 128)]


def diagonal(product, rows, entries):
    _, col = iotas((rows, product.shape[1]))
    kept = product[0:rows]
    for k in range(1, entries):
        kept = jnp.where((col & (entries - 1)) == k, product[rows * k : rows * k + rows], kept)
    return kept


def spread_matrix():
    row, col = iotas((128, 512))
    return ones_where(((row >> 5) == (col >> 7)) & ((row & 31) == (col & 31)))


def place_matrix(j):
    row, col = iotas((128, 512))
    return ones_where(((row >> 5) == (col >> 7)) & ((col & 127) == (j * 32 + (row & 31))))


def kernel(
    points_h,
    basis_h,
    transfer_h,
    far_h,
    near_h,
    near_leaf_h,
    near_count_h,
    far_slots_h,
    far_count_h,
    recv_h,
    coarse_h,
    coarse_far_h,
    coarse_count_h,
    out_ref,
    pts,
    bas,
    trn,
    farv,
    nearv,
    cb,
    halo,
    p1,
    rown,
    pw,
    tp,
    r2,
    send,
    fbuf,
    tt,
    bx,
    tn,
    nr,
    nf,
    fr,
    dr,
    idxv,
    idxs,
    nls,
    ncs,
    fss,
    fcs,
    cfs,
    ccs,
    load_sem,
    idx_ssem,
    idx_rsem,
    p1_ssem,
    p1_rsem,
    p2_ssem,
    p2_rsem,
    pw_ssem,
    pw_rsem,
    halo_ssem,
    halo_rsem,
    cb_ssem,
    cb_rsem,
):
    me = lax.axis_index("leaf")
    grp = lax.axis_index("grp")
    core = lax.rem(me, 2)
    y = lax.rem(lax.div(me, 2), 8)
    z = lax.div(me, 16)
    in_group = lax.rem(me, 16)
    place = (1 - core) * z + core * y
    line = (1 - core) * y + core * z
    own_server = core * 8 + line
    own_client = line * 2 + core

    def line_peer(o):
        turned = lax.rem(place + o, 8)
        return ((1 - core) * (turned * 16 + y * 2) + core * (z * 16 + turned * 2 + 1), grp)

    def server(m):
        kind, at = lax.div(m, 8), lax.rem(m, 8)
        return ((1 - kind) * (z * 16 + at * 2) + kind * (at * 16 + y * 2 + 1), grp)

    def client_slot(m):
        kind = lax.div(m, 8)
        return ((1 - kind) * y + kind * z) * 2 + core

    def client(slot):
        at, c = lax.div(slot, 2), lax.rem(slot, 2)
        return ((1 - core) * (z * 16 + at * 2) + core * (at * 16 + y * 2) + c, grp)

    def group_peer(o):
        return (z * 16 + lax.rem(in_group + o, 16), grp)

    def column_peer(o):
        turned = lax.rem(z + (o >> 1), 8)
        return (turned * 16 + y * 2 + lax.rem(core + (o & 1), 2), grp)

    up = (lax.rem(me + 1, 128), grp)
    down = (lax.rem(me + 127, 128), grp)

    def grp_peer(o):
        return (me, lax.rem(grp + o, 4))

    loads = {}

    def load(name, src, dst, n):
        loads[name] = pltpu.make_async_copy(src, dst, load_sem.at[n])
        loads[name].start()

    load("points", points_h, pts, 0)
    load("basis", basis_h, bas, 1)
    load("transfer", transfer_h, trn, 2)
    load("recv", recv_h, idxv.at[own_client], 3)
    load("coarse", coarse_h, cb.at[grp], 4)

    barrier = pltpu.get_barrier_semaphore()
    peers = [group_peer(o) for o in range(1, 16)]
    peers += [column_peer(o) for o in range(2, 16)]
    peers += [up, down]
    peers += [grp_peer(o) for o in range(1, 4)]
    for peer in peers:
        pl.semaphore_signal(barrier, inc=1, device_id=peer, device_id_type=MESH)

    load("near_leaf", near_leaf_h, nls, 5)
    load("near_count", near_count_h, ncs, 6)
    load("far_slots", far_slots_h, fss, 7)
    load("far_count", far_count_h, fcs, 8)
    load("coarse_far", coarse_far_h, cfs, 9)
    load("coarse_count", coarse_count_h, ccs, 10)
    load("near", near_h, nearv, 11)
    load("far", far_h, farv, 12)

    loads["points"].wait()
    loads["basis"].wait()
    _, col = iotas((32, 256))
    quad_masks = [ones_where((col >> 6) == l4) for l4 in range(4)]
    for quad in range(8):
        lanes = slice(256 * quad, 256 * quad + 256)
        v = bas[:, lanes]
        vv = jnp.concatenate([v * mask for mask in quad_masks], axis=0)
        p1[place, quad] = dot_nt(pts[:, lanes], vv).astype(BF)

    loads["recv"].wait()
    loads["coarse"].wait()
    pl.semaphore_wait(barrier, len(peers))

    sends = []

    def remote(src, dst, ssem, rsem, peer):
        copy = pltpu.make_async_remote_copy(
            src_ref=src,
            dst_ref=dst,
            send_sem=ssem,
            recv_sem=rsem,
            device_id=peer,
            device_id_type=MESH,
        )
        copy.start()
        sends.append(copy)
        return copy

    p1_copies = [
        remote(
            p1.at[place],
            p1.at[place],
            p1_ssem.at[o],
            p1_rsem.at[o],
            line_peer(o),
        )
        for o in range(1, 8)
    ]
    idx_copies = []
    for o in range(1, 16):
        m = lax.rem(own_server + o, 16)
        slot = client_slot(m)
        idx_copies.append(
            remote(
                idxv.at[own_client],
                idxv.at[slot],
                idx_ssem.at[o],
                idx_rsem.at[slot],
                server(m),
            )
        )
    halo_copies = [
        remote(pts.at[:, pl.ds(1792, 256)], halo.at[0], halo_ssem.at[0], halo_rsem.at[0], up),
        remote(pts.at[:, pl.ds(0, 256)], halo.at[1], halo_ssem.at[1], halo_rsem.at[1], down),
    ]
    cb_copies = [
        remote(cb.at[grp], cb.at[grp], cb_ssem.at[o], cb_rsem.at[o], grp_peer(o))
        for o in range(1, 4)
    ]

    spread = spread_matrix()
    wide = dot_nn(p1[place].reshape(128, 128), spread).astype(BF)
    for quad in range(8):
        for a in range(4):
            rown[4 * quad + a] = wide[16 * quad : 16 * quad + 16, 128 * a : 128 * a + 128]
    loads["transfer"].wait()
    total = jnp.zeros((16, 128), F32)
    row, col = iotas((256, 128))
    for c in range(4):
        ex = expand(lane_tiles(trn[8 * c : 8 * c + 8, :].astype(F32)))
        product = dot_nt(rown[8 * c : 8 * c + 8].reshape(128, 128), ex)
        kept = diagonal(product, 16, 8).astype(BF)
        total += dot_nn(kept, ones_where(col == c * 32 + (row >> 3)))
    pw[in_group] = total.astype(BF)

    pw_copies = [
        remote(pw.at[in_group], pw.at[in_group], pw_ssem.at[o], pw_rsem.at[o], group_peer(o))
        for o in range(1, 16)
    ]

    loads["far"].wait()
    loads["far_count"].wait()

    def prepare(l, _):
        count = fcs[0, l]
        sub, _ = iotas((8, 128))
        low = jnp.where(sub < count, 1.0, 0.0)
        high = jnp.where(sub + 8 < count, 1.0, 0.0)
        blocks = farv[l].astype(F32)
        bx[l, :, 0:128] = expand([tile * low for tile in lane_tiles(blocks[0:8])])
        bx[l, :, 128:256] = expand([tile * high for tile in lane_tiles(blocks[8:16])])
        return 0

    lax.fori_loop(0, 32, prepare, 0)

    _, col = iotas((16, 128))
    left = jnp.where(col < 64, 1.0, 0.0)
    right = 1.0 - left

    def near_table(m, tile):
        value = tile.astype(F32)
        turned = pltpu.roll(value, 64, 1)
        tn[m] = jnp.concatenate([value * left, turned * right], axis=0).astype(BF)
        tn[m + 1] = jnp.concatenate([turned * left, value * right], axis=0).astype(BF)

    for j in range(16):
        near_table(4 + 2 * j, pts[:, 128 * j : 128 * j + 128])
    for copy in halo_copies:
        copy.wait_recv()
    for j in range(2):
        near_table(2 * j, halo[0, :, 128 * j : 128 * j + 128])
        near_table(36 + 2 * j, halo[1, :, 128 * j : 128 * j + 128])
    loads["near"].wait()
    loads["near_leaf"].wait()
    loads["near_count"].wait()

    def near_pair(j, _):
        _, lane = iotas((32, 256))
        for l2 in range(2):
            l = 2 * j + l2
            blocks = nearv[l].astype(F32)
            flat = jnp.concatenate(lane_tiles(blocks), axis=0).astype(BF)
            source = jnp.concatenate(
                [tn[jnp.clip(nls[k, l] - me * 32 + 4, 0, 39)] for k in range(8)], axis=0
            )
            kept = diagonal(dot_nt(source, flat), 32, 8)
            kept = jnp.where((lane & 7) < ncs[0, l], kept, 0.0)
            high = kept.astype(BF)
            for part, value in enumerate([high, (kept - high.astype(F32)).astype(BF)]):
                nr[part, j, :, 512 * l2 : 512 * l2 + 256] = value[0:16]
                nr[part, j, :, 512 * l2 + 256 : 512 * l2 + 512] = value[16:32]
        return 0

    lax.fori_loop(0, 8, near_pair, 0)

    for copy in p1_copies:
        copy.wait_recv()
    for o in range(1, 16):
        slot = lax.rem(own_client + o, 16)
        pltpu.make_async_copy(idxv.at[slot], idxv.at[slot], idx_rsem.at[slot]).wait()
    to_smem = pltpu.make_async_copy(idxv, idxs, load_sem.at[13])
    to_smem.start()
    for j in range(4):
        place_j = place_matrix(j)
        for g in range(2):
            m = 4 * g + j
            wide = dot_nn(p1[m].reshape(128, 128), place_j).astype(BF)
            for quad in range(8):
                for a in range(4):
                    r2[32 * m + 4 * quad + a] = wide[
                        16 * quad : 16 * quad + 16, 128 * a : 128 * a + 128
                    ]
    to_smem.wait()
    first = (1 - core) * (y * 2) + core * (z * 16 + 1)
    stride = (1 - core) * 16 + core * 2
    p2_copies = []
    for o in list(range(1, 16)) + [0]:
        slot = lax.rem(own_client + o, 16)
        for g in range(2):
            tile = r2[32 * (4 * g) + idxs[slot, 0, first + 4 * g * stride]]
            for j in range(1, 4):
                m = 4 * g + j
                tile = tile + r2[32 * m + idxs[slot, 0, first + m * stride]]
            if o == 0:
                fbuf[own_server, g] = tile
            else:
                send[o, g] = tile
        if o:
            p2_copies.append(
                remote(
                    send.at[o],
                    fbuf.at[own_server],
                    p2_ssem.at[o],
                    p2_rsem.at[own_server],
                    client(slot),
                )
            )

    lax.fori_loop(8, 16, near_pair, 0)
    row, col = iotas((1024, 128))
    group = row >> 8
    fold_near = ones_where(col == (group >> 1) * 64 + ((row & 255) >> 3) * 2 + (group & 1))
    nf[...] = dot_nn(nr[0].reshape(256, 1024), fold_near)
    nf[...] += dot_nn(nr[1].reshape(256, 1024), fold_near)

    for copy in pw_copies:
        copy.wait_recv()
    wide = dot_nn(pw[...].reshape(256, 128), spread).astype(BF)
    for device in range(16):
        for c in range(4):
            tp[4 * device + c] = wide[16 * device : 16 * device + 16, 128 * c : 128 * c + 128]
    for copy in cb_copies:
        copy.wait_recv()
    loads["coarse_far"].wait()
    loads["coarse_count"].wait()
    total = jnp.zeros((16, 128), F32)
    sub, _ = iotas((8, 1024))
    row, col = iotas((256, 128))
    for cp in range(2):
        counts = jnp.where(sub < 4, ccs[0, 2 * cp], ccs[0, 2 * cp + 1])
        product = jnp.zeros((128, 256), F32)
        for gp in range(2):
            halves = []
            for g in (2 * gp, 2 * gp + 1):
                rows = jnp.concatenate(
                    [cb[g, 2 * cp].astype(F32), cb[g, 2 * cp + 1].astype(F32)], axis=0
                )
                rows = jnp.where((sub & 3) + 4 * g < counts, rows, 0.0)
                halves.append(expand(lane_tiles(rows)))
            weights = jnp.concatenate(halves, axis=1)
            source = jnp.concatenate(
                [
                    jnp.concatenate(
                        [
                            tp[cfs[2 * cp + (k >> 2), 4 * g + (k & 3)] & 63]
                            for g in (2 * gp, 2 * gp + 1)
                        ],
                        axis=1,
                    )
                    for k in range(8)
                ],
                axis=0,
            )
            product += dot_nt(source, weights)
        kept = diagonal(product, 16, 8).astype(BF)
        target = (2 * cp + ((row & 7) >> 2)) * 32 + (row >> 3)
        total += dot_nn(kept, ones_where(col == target))
    field = total.astype(BF)

    row, col = iotas((128, 256))
    flat = jnp.concatenate(lane_tiles(trn[...]), axis=0)
    spreads = []
    for r4 in range(4):
        hit = ((row >> 5) == ((col & 31) >> 3)) & (((row & 31) >> 2) == (col >> 5))
        spreads.append(dot_nn(field, ones_where(hit & ((row & 3) == r4))).astype(BF))
    _, lane = iotas((16, 256))
    _, col = iotas((16, 128))
    for part in range(4):
        pieces = []
        for l in range(8 * part, 8 * part + 8):
            mask = ones_where((lane & 31) == l)
            pieces += [spreads[r4] * mask for r4 in range(4)]
        product = dot_nn(jnp.concatenate(pieces, axis=0), flat)
        for i in range(8):
            kept = product[64 * i : 64 * i + 16]
            for r4 in range(1, 4):
                at = 64 * i + 16 * r4
                kept = jnp.where((col >> 5) == r4, product[at : at + 16], kept)
            dr[8 * part + i] = kept.astype(BF)

    loads["far_slots"].wait()
    for o in range(1, 16):
        m = lax.rem(own_server + o, 16)
        pltpu.make_async_copy(fbuf.at[m], fbuf.at[m], p2_rsem.at[m]).wait()
    wide = dot_nn(fbuf[...].reshape(512, 128), spread).astype(BF)
    for m in range(16):
        for i in range(8):
            kind, at = divmod(m, 8)
            f = at * 16 + i * 2 + 1 if kind else i * 16 + at * 2
            row = 32 * m + 16 * (i // 4)
            lane = 128 * (i % 4)
            tt[f] = wide[row : row + 16, lane : lane + 128]

    def far_part(step, _):
        for i in range(4):
            l = 4 * step + i
            source = jnp.concatenate(
                [
                    jnp.concatenate([tt[fss[k, l]], tt[fss[k + 8, l]]], axis=1)
                    for k in range(8)
                ],
                axis=0,
            )
            fr[l] = diagonal(dot_nt(source, bx[l]), 16, 8).astype(BF)
        return 0

    lax.fori_loop(0, 8, far_part, 0)

    row, col = iotas((256, 32))
    local = dot_nn(fr[...].reshape(512, 256), ones_where(col == (row >> 3)))
    row, col = iotas((128, 32))
    local += dot_nn(dr[...].reshape(512, 128), ones_where(col == (row & 31)))
    local = local.astype(BF)
    _, col = iotas((16, 128))
    for j in range(16):
        both = dot_nn(local[32 * j : 32 * j + 32], bas[:, 128 * j : 128 * j + 128])
        field = jnp.where(col < 64, both[0:16], both[16:32])
        out_ref[:, 128 * j : 128 * j + 128] = (field + nf[16 * j : 16 * j + 16]).astype(BF)

    for copy in sends:
        copy.wait_send()


def per_device(
    points_in,
    leaf_basis,
    transfer,
    far_blocks,
    near_blocks,
    near_leaf,
    near_count,
    far_slots,
    far_count,
    recv_rows,
    coarse_blocks,
    coarse_far,
    coarse_count,
):
    vmem = pltpu.VMEM
    smem = pltpu.SMEM
    dma = pltpu.SemaphoreType.DMA
    anywhere = pl.BlockSpec(memory_space=pltpu.HBM)
    return pl.pallas_call(
        kernel,
        out_shape=jax.ShapeDtypeStruct((16, 2048), BF),
        in_specs=[anywhere] * 13,
        out_specs=pl.BlockSpec(memory_space=pltpu.VMEM),
        scratch_shapes=[
            vmem((16, 2048), BF),
            vmem((32, 2048), BF),
            vmem((32, 1024), BF),
            vmem((32, 16, 1024), BF),
            vmem((32, 8, 4096), BF),
            vmem((4, 4, 4, 1024), BF),
            vmem((2, 16, 256), BF),
            vmem((8, 8, 16, 128), BF),
            vmem((32, 16, 128), BF),
            vmem((16, 16, 128), BF),
            vmem((64, 16, 128), BF),
            vmem((256, 16, 128), BF),
            vmem((16, 2, 16, 128), BF),
            vmem((16, 2, 16, 128), BF),
            vmem((128, 16, 128), BF),
            vmem((32, 256, 256), BF),
            vmem((40, 32, 128), BF),
            vmem((2, 16, 16, 1024), BF),
            vmem((256, 128), F32),
            vmem((32, 16, 256), BF),
            vmem((32, 16, 128), BF),
            vmem((16, 1, 128), jnp.int32),
            smem((16, 1, 128), jnp.int32),
            smem((8, 32), jnp.int32),
            smem((1, 32), jnp.int32),
            smem((16, 32), jnp.int32),
            smem((1, 32), jnp.int32),
            smem((4, 16), jnp.int32),
            smem((1, 4), jnp.int32),
            dma((14,)),
            dma((16,)),
            dma((16,)),
            dma((8,)),
            dma((8,)),
            dma((16,)),
            dma((16,)),
            dma((16,)),
            dma((16,)),
            dma((2,)),
            dma((2,)),
            dma((4,)),
            dma((4,)),
        ],
        compiler_params=pltpu.CompilerParams(
            collective_id=0, has_side_effects=True, vmem_limit_bytes=63 * 1024 * 1024
        ),
        cost_estimate=pl.CostEstimate(
            flops=60_000_000, bytes_accessed=3_600_000, transcendentals=0
        ),
    )(
        points_in,
        leaf_basis,
        transfer,
        far_blocks,
        near_blocks,
        near_leaf.T,
        near_count.reshape(1, 32),
        far_slots.T,
        far_count.reshape(1, 32),
        recv_rows.reshape(1, 128),
        coarse_blocks,
        coarse_far,
        coarse_count.reshape(1, 4),
    )


def solution(mesh):
    in_specs = (
        P("grp", "leaf"),
        P(None, "leaf"),
        P("leaf", None),
        P("leaf", None, None),
        P("leaf", None, None),
        P("leaf", None),
        P("leaf"),
        P("leaf", None),
        P("leaf"),
        P("leaf", None, None),
        P("leaf", "grp", None),
        P("leaf", None),
        P("leaf"),
    )
    out_specs = P("grp", "leaf")
    return jax.shard_map(
        per_device, mesh=mesh, in_specs=in_specs, out_specs=out_specs, check_vma=False
    )
```

```python
import jax
import jax.numpy as jnp
from jax import lax
from jax.experimental import pallas as pl
from jax.experimental.pallas import tpu as pltpu
from jax.sharding import PartitionSpec as P

BF = jnp.bfloat16
F32 = jnp.float32
MESH = pl.DeviceIdType.MESH


def dot_nt(a, b):
    return lax.dot_general(a, b, (((1,), (1,)), ((), ())), preferred_element_type=F32)


def dot_nn(a, b):
    return jnp.dot(a, b, preferred_element_type=F32)


def iotas(shape):
    row = lax.broadcasted_iota(jnp.int32, shape, 0)
    col = lax.broadcasted_iota(jnp.int32, shape, 1)
    return row, col


def ones_where(cond):
    return jnp.where(cond, 1.0, 0.0).astype(BF)


def expand(tiles):
    _, col = iotas((8, 128))
    masks = [jnp.where((col >> 5) == r4, 1.0, 0.0) for r4 in range(4)]
    return jnp.concatenate([tile * mask for tile in tiles for mask in masks], axis=0).astype(BF)


def lane_tiles(value):
    return [value[:, 128 * t : 128 * t + 128] for t in range(value.shape[1] // 128)]


def diagonal(product, rows, entries):
    _, col = iotas((rows, product.shape[1]))
    kept = product[0:rows]
    for k in range(1, entries):
        kept = jnp.where((col & (entries - 1)) == k, product[rows * k : rows * k + rows], kept)
    return kept


def spread_matrix():
    row, col = iotas((128, 512))
    return ones_where(((row >> 5) == (col >> 7)) & ((row & 31) == (col & 31)))


def place_matrix(j):
    row, col = iotas((128, 512))
    return ones_where(((row >> 5) == (col >> 7)) & ((col & 127) == (j * 32 + (row & 31))))


def kernel(
    points_h,
    basis_h,
    transfer_h,
    far_h,
    near_h,
    near_leaf_h,
    near_count_h,
    far_slots_h,
    far_count_h,
    recv_h,
    coarse_h,
    coarse_far_h,
    coarse_count_h,
    out_ref,
    pts,
    bas,
    trn,
    farv,
    nearv,
    cb,
    halo,
    p1,
    rown,
    pw,
    tp,
    r2,
    send,
    fbuf,
    tt,
    wf,
    vf,
    bs,
    tn,
    nr,
    nf,
    dr,
    dn,
    idxv,
    idxs,
    nls,
    ncs,
    fss,
    fcs,
    cfs,
    ccs,
    load_sem,
    idx_ssem,
    idx_rsem,
    p1_ssem,
    p1_rsem,
    p2_ssem,
    p2_rsem,
    pw_ssem,
    pw_rsem,
    halo_ssem,
    halo_rsem,
    cb_ssem,
    cb_rsem,
):
    me = lax.axis_index("leaf")
    grp = lax.axis_index("grp")
    core = lax.rem(me, 2)
    y = lax.rem(lax.div(me, 2), 8)
    z = lax.div(me, 16)
    in_group = lax.rem(me, 16)
    place = (1 - core) * z + core * y
    line = (1 - core) * y + core * z
    own_server = core * 8 + line
    own_client = line * 2 + core

    def line_peer(o):
        turned = lax.rem(place + o, 8)
        return ((1 - core) * (turned * 16 + y * 2) + core * (z * 16 + turned * 2 + 1), grp)

    def server(m):
        kind, at = lax.div(m, 8), lax.rem(m, 8)
        return ((1 - kind) * (z * 16 + at * 2) + kind * (at * 16 + y * 2 + 1), grp)

    def client_slot(m):
        kind = lax.div(m, 8)
        return ((1 - kind) * y + kind * z) * 2 + core

    def client(slot):
        at, c = lax.div(slot, 2), lax.rem(slot, 2)
        return ((1 - core) * (z * 16 + at * 2) + core * (at * 16 + y * 2) + c, grp)

    def group_peer(o):
        return (z * 16 + lax.rem(in_group + o, 16), grp)

    def column_peer(o):
        turned = lax.rem(z + (o >> 1), 8)
        return (turned * 16 + y * 2 + lax.rem(core + (o & 1), 2), grp)

    up = (lax.rem(me + 1, 128), grp)
    down = (lax.rem(me + 127, 128), grp)

    def grp_peer(o):
        return (me, lax.rem(grp + o, 4))

    loads = {}

    def load(name, src, dst, n):
        loads[name] = pltpu.make_async_copy(src, dst, load_sem.at[n])
        loads[name].start()

    load("points", points_h, pts, 0)
    load("basis", basis_h, bas, 1)
    load("transfer", transfer_h, trn, 2)
    load("recv", recv_h, idxv.at[own_client], 3)
    load("coarse", coarse_h, cb.at[grp], 4)

    barrier = pltpu.get_barrier_semaphore()
    peers = [group_peer(o) for o in range(1, 16)]
    peers += [column_peer(o) for o in range(2, 16)]
    peers += [up, down]
    peers += [grp_peer(o) for o in range(1, 4)]
    for peer in peers:
        pl.semaphore_signal(barrier, inc=1, device_id=peer, device_id_type=MESH)

    load("near_leaf", near_leaf_h, nls, 5)
    load("near_count", near_count_h, ncs, 6)
    load("far_slots", far_slots_h, fss, 7)
    load("far_count", far_count_h, fcs, 8)
    load("coarse_far", coarse_far_h, cfs, 9)
    load("coarse_count", coarse_count_h, ccs, 10)
    load("far", far_h, farv, 12)
    load("near", near_h, nearv, 11)

    loads["points"].wait()
    loads["basis"].wait()
    _, col = iotas((32, 256))
    quad_masks = [ones_where((col >> 6) == l4) for l4 in range(4)]
    for quad in range(8):
        lanes = slice(256 * quad, 256 * quad + 256)
        v = bas[:, lanes]
        vv = jnp.concatenate([v * mask for mask in quad_masks], axis=0)
        p1[0, quad] = dot_nt(pts[:, lanes], vv).astype(BF)

    loads["recv"].wait()
    loads["coarse"].wait()
    def prepare(quad, _):
        sub, _ = iotas((16, 1024))
        for l4 in range(4):
            l = 4 * quad + l4
            blocks = jnp.where(sub < fcs[0, l], farv[l].astype(F32), 0.0)
            for t, tile in enumerate(lane_tiles(blocks)):
                bs[pl.ds((8 * l4 + t) * 16, 16), :] = tile
        _, col = iotas((32, 128))
        masks = [jnp.where((col >> 5) == r4, 1.0, 0.0) for r4 in range(4)]
        row, col = iotas((32, 128))
        gather = ones_where((col & 31) == row)
        for k in range(16):
            tile = bs[pl.ds(k, 32, stride=16), :]
            rows = jnp.concatenate([tile * mask for mask in masks], axis=0).astype(BF)
            wf[quad, 32 * k : 32 * k + 32, :] = dot_nt(gather, rows).astype(BF)
        return 0

    def prepare_all():
        loads["far"].wait()
        loads["far_count"].wait()
        lax.fori_loop(0, 8, prepare, 0)
        row, col = iotas((128, 32))
        permute = ones_where(col == 4 * (row & 7) + (row >> 5))
        row, col = iotas((128, 256))
        block = ((row >> 3) & 3) == (col >> 6)
        for quad in range(8):
            rows = dot_nn(permute, bas[:, 256 * quad : 256 * quad + 256])
            vf[quad] = jnp.where(block, rows, 0.0).astype(BF)

    @pl.when(z < 4)
    def _():
        prepare_all()

    pl.semaphore_wait(barrier, len(peers))

    sends = []

    def remote(src, dst, ssem, rsem, peer):
        copy = pltpu.make_async_remote_copy(
            src_ref=src,
            dst_ref=dst,
            send_sem=ssem,
            recv_sem=rsem,
            device_id=peer,
            device_id_type=MESH,
        )
        copy.start()
        sends.append(copy)
        return copy

    p1_copies = {
        8 - o: remote(
            p1.at[0],
            p1.at[8 - o],
            p1_ssem.at[o],
            p1_rsem.at[8 - o],
            line_peer(o),
        )
        for o in (4, 3, 5, 2, 6, 1, 7)
    }
    idx_copies = []
    for o in range(1, 16):
        m = lax.rem(own_server + o, 16)
        slot = client_slot(m)
        idx_copies.append(
            remote(
                idxv.at[own_client],
                idxv.at[slot],
                idx_ssem.at[o],
                idx_rsem.at[slot],
                server(m),
            )
        )
    halo_copies = [
        remote(pts.at[:, pl.ds(1792, 256)], halo.at[0], halo_ssem.at[0], halo_rsem.at[0], up),
        remote(pts.at[:, pl.ds(0, 256)], halo.at[1], halo_ssem.at[1], halo_rsem.at[1], down),
    ]
    cb_copies = [
        remote(cb.at[grp], cb.at[grp], cb_ssem.at[o], cb_rsem.at[o], grp_peer(o))
        for o in range(1, 4)
    ]

    spread = spread_matrix()
    wide = dot_nn(p1[0].reshape(128, 128), spread).astype(BF)
    for quad in range(8):
        for a in range(4):
            rown[4 * quad + a] = wide[16 * quad : 16 * quad + 16, 128 * a : 128 * a + 128]
    loads["transfer"].wait()
    total = jnp.zeros((16, 128), F32)
    row, col = iotas((256, 128))
    for c in range(4):
        ex = expand(lane_tiles(trn[8 * c : 8 * c + 8, :].astype(F32)))
        product = dot_nt(rown[8 * c : 8 * c + 8].reshape(128, 128), ex)
        kept = diagonal(product, 16, 8).astype(BF)
        total += dot_nn(kept, ones_where(col == c * 32 + (row >> 3)))
    pw[in_group] = total.astype(BF)

    pw_copies = [
        remote(pw.at[in_group], pw.at[in_group], pw_ssem.at[o], pw_rsem.at[o], group_peer(o))
        for o in range(1, 16)
    ]

    @pl.when(z >= 4)
    def _():
        prepare_all()

    _, col = iotas((16, 128))
    left = jnp.where(col < 64, 1.0, 0.0)
    right = 1.0 - left

    def near_table(m, tile):
        value = tile.astype(F32)
        turned = pltpu.roll(value, 64, 1)
        tn[m] = jnp.concatenate([value * left, turned * right], axis=0).astype(BF)
        tn[m + 1] = jnp.concatenate([turned * left, value * right], axis=0).astype(BF)

    for j in range(16):
        near_table(4 + 2 * j, pts[:, 128 * j : 128 * j + 128])
    for copy in halo_copies:
        copy.wait_recv()
    for j in range(2):
        near_table(2 * j, halo[0, :, 128 * j : 128 * j + 128])
        near_table(36 + 2 * j, halo[1, :, 128 * j : 128 * j + 128])
    loads["near"].wait()
    loads["near_leaf"].wait()
    loads["near_count"].wait()

    def near_pair(j, _):
        _, lane = iotas((32, 256))
        for l2 in range(2):
            l = 2 * j + l2
            blocks = nearv[l].astype(F32)
            flat = jnp.concatenate(lane_tiles(blocks), axis=0).astype(BF)
            source = jnp.concatenate(
                [tn[jnp.clip(nls[k, l] - me * 32 + 4, 0, 39)] for k in range(8)], axis=0
            )
            kept = diagonal(dot_nt(source, flat), 32, 8)
            kept = jnp.where((lane & 7) < ncs[0, l], kept, 0.0)
            high = kept.astype(BF)
            for part, value in enumerate([high, (kept - high.astype(F32)).astype(BF)]):
                nr[part, j, :, 512 * l2 : 512 * l2 + 256] = value[0:16]
                nr[part, j, :, 512 * l2 + 256 : 512 * l2 + 512] = value[16:32]
        return 0

    lax.fori_loop(0, 8, near_pair, 0)

    for o in range(1, 16):
        slot = lax.rem(own_client + o, 16)
        pltpu.make_async_copy(idxv.at[slot], idxv.at[slot], idx_rsem.at[slot]).wait()
    to_smem = pltpu.make_async_copy(idxv, idxs, load_sem.at[13])
    to_smem.start()
    for i in (0, 1, 2, 3, 7, 5, 4, 6):
        if i:
            p1_copies[i].wait_recv()
        wide = dot_nn(p1[i].reshape(128, 128), place_matrix(i % 4)).astype(BF)
        for quad in range(8):
            for a in range(4):
                r2[32 * i + 4 * quad + a] = wide[
                    16 * quad : 16 * quad + 16, 128 * a : 128 * a + 128
                ]
    to_smem.wait()
    owners = []
    for i in range(8):
        turned = lax.rem(place + i, 8)
        owners.append((1 - core) * (turned * 16 + y * 2) + core * (z * 16 + turned * 2 + 1))
    p2_copies = []
    for o in (8, 9, 7, 10, 6, 11, 5, 12, 4, 13, 3, 14, 2, 15, 1, 0):
        slot = lax.rem(own_client + o, 16)
        for g in range(2):
            tile = r2[32 * (4 * g) + idxs[slot, 0, owners[4 * g]]]
            for j in range(1, 4):
                m = 4 * g + j
                tile = tile + r2[32 * m + idxs[slot, 0, owners[m]]]
            if o == 0:
                fbuf[own_server, g] = tile
            else:
                send[o, g] = tile
        if o:
            p2_copies.append(
                remote(
                    send.at[o],
                    fbuf.at[own_server],
                    p2_ssem.at[o],
                    p2_rsem.at[own_server],
                    client(slot),
                )
            )

    lax.fori_loop(8, 16, near_pair, 0)
    row, col = iotas((1024, 128))
    group = row >> 8
    fold_near = ones_where(col == (group >> 1) * 64 + ((row & 255) >> 3) * 2 + (group & 1))
    nf[...] = dot_nn(nr[0].reshape(256, 1024), fold_near)
    nf[...] += dot_nn(nr[1].reshape(256, 1024), fold_near)

    for copy in pw_copies:
        copy.wait_recv()
    wide = dot_nn(pw[...].reshape(256, 128), spread).astype(BF)
    for device in range(16):
        for c in range(4):
            tp[4 * device + c] = wide[16 * device : 16 * device + 16, 128 * c : 128 * c + 128]
    for copy in cb_copies:
        copy.wait_recv()
    loads["coarse_far"].wait()
    loads["coarse_count"].wait()
    total = jnp.zeros((16, 128), F32)
    sub, _ = iotas((8, 1024))
    row, col = iotas((256, 128))
    for cp in range(2):
        counts = jnp.where(sub < 4, ccs[0, 2 * cp], ccs[0, 2 * cp + 1])
        product = jnp.zeros((128, 256), F32)
        for gp in range(2):
            halves = []
            for g in (2 * gp, 2 * gp + 1):
                rows = jnp.concatenate(
                    [cb[g, 2 * cp].astype(F32), cb[g, 2 * cp + 1].astype(F32)], axis=0
                )
                rows = jnp.where((sub & 3) + 4 * g < counts, rows, 0.0)
                halves.append(expand(lane_tiles(rows)))
            weights = jnp.concatenate(halves, axis=1)
            source = jnp.concatenate(
                [
                    jnp.concatenate(
                        [
                            tp[cfs[2 * cp + (k >> 2), 4 * g + (k & 3)] & 63]
                            for g in (2 * gp, 2 * gp + 1)
                        ],
                        axis=1,
                    )
                    for k in range(8)
                ],
                axis=0,
            )
            product += dot_nt(source, weights)
        kept = diagonal(product, 16, 8).astype(BF)
        target = (2 * cp + ((row & 7) >> 2)) * 32 + (row >> 3)
        total += dot_nn(kept, ones_where(col == target))
    field = total.astype(BF)

    row, col = iotas((128, 256))
    flat = jnp.concatenate(lane_tiles(trn[...]), axis=0)
    spreads = []
    for r4 in range(4):
        hit = ((row >> 5) == ((col & 31) >> 3)) & (((row & 31) >> 2) == (col >> 5))
        spreads.append(dot_nn(field, ones_where(hit & ((row & 3) == r4))).astype(BF))
    _, lane = iotas((16, 256))
    _, col = iotas((16, 128))
    for part in range(4):
        pieces = []
        for l in range(8 * part, 8 * part + 8):
            mask = ones_where((lane & 31) == l)
            pieces += [spreads[r4] * mask for r4 in range(4)]
        product = dot_nn(jnp.concatenate(pieces, axis=0), flat)
        for i in range(8):
            kept = product[64 * i : 64 * i + 16]
            for r4 in range(1, 4):
                at = 64 * i + 16 * r4
                kept = jnp.where((col >> 5) == r4, product[at : at + 16], kept)
            l = 8 * part + i
            dr[l // 4, :, 128 * (l % 4) : 128 * (l % 4) + 128] = kept.astype(BF)
    row, col = iotas((512, 128))
    hit = ((row >> 7) == ((col >> 3) & 3)) & ((row & 31) == 4 * (col & 7) + (col >> 5))
    dn[...] = dot_nn(dr[...].reshape(128, 512), ones_where(hit))

    loads["far_slots"].wait()
    for o in range(16):
        m = lax.rem(own_server + o, 16)
        if o:
            pltpu.make_async_copy(fbuf.at[m], fbuf.at[m], p2_rsem.at[m]).wait()
        kind, at = lax.div(m, 8), lax.rem(m, 8)
        wide = dot_nn(fbuf[m].reshape(32, 128), spread).astype(BF)
        for i in range(8):
            row_owner = lax.rem(z + i, 8) * 16 + at * 2
            column_owner = at * 16 + lax.rem(y + i, 8) * 2 + 1
            f = (1 - kind) * row_owner + kind * column_owner
            row, lane = 16 * (i // 4), 128 * (i % 4)
            tt[f] = wide[row : row + 16, lane : lane + 128]
    _, col = iotas((16, 128))
    parts = [ones_where((col >> 5) == j) for j in range(4)]
    for quad in range(8):
        rows = []
        for l in range(4 * quad, 4 * quad + 4):
            tiles = []
            for k in range(0, 16, 4):
                tile = tt[fss[k, l]] * parts[0]
                for j in range(1, 4):
                    tile = tile + tt[fss[k + j, l]] * parts[j]
                tiles.append(tile)
            rows.append(jnp.concatenate(tiles, axis=1))
        product = dot_nn(jnp.concatenate(rows, axis=0), wf[quad])
        local = product[0:16]
        for l4 in range(1, 4):
            local = jnp.where(((col >> 3) & 3) == l4, product[16 * l4 : 16 * l4 + 16], local)
        local = (local + dn[16 * quad : 16 * quad + 16]).astype(BF)
        near = jnp.concatenate(
            [nf[32 * quad : 32 * quad + 16], nf[32 * quad + 16 : 32 * quad + 32]], axis=1
        )
        out_ref[:, 256 * quad : 256 * quad + 256] = (dot_nn(local, vf[quad]) + near).astype(BF)

    for copy in sends:
        copy.wait_send()


def per_device(
    points_in,
    leaf_basis,
    transfer,
    far_blocks,
    near_blocks,
    near_leaf,
    near_count,
    far_slots,
    far_count,
    recv_rows,
    coarse_blocks,
    coarse_far,
    coarse_count,
):
    vmem = pltpu.VMEM
    smem = pltpu.SMEM
    dma = pltpu.SemaphoreType.DMA
    anywhere = pl.BlockSpec(memory_space=pltpu.HBM)
    return pl.pallas_call(
        kernel,
        out_shape=jax.ShapeDtypeStruct((16, 2048), BF),
        in_specs=[anywhere] * 13,
        out_specs=pl.BlockSpec(memory_space=pltpu.VMEM),
        scratch_shapes=[
            vmem((16, 2048), BF),
            vmem((32, 2048), BF),
            vmem((32, 1024), BF),
            vmem((32, 16, 1024), BF),
            vmem((32, 8, 4096), BF),
            vmem((4, 4, 4, 1024), BF),
            vmem((2, 16, 256), BF),
            vmem((8, 8, 16, 128), BF),
            vmem((32, 16, 128), BF),
            vmem((16, 16, 128), BF),
            vmem((64, 16, 128), BF),
            vmem((256, 16, 128), BF),
            vmem((16, 2, 16, 128), BF),
            vmem((16, 2, 16, 128), BF),
            vmem((128, 16, 128), BF),
            vmem((8, 512, 128), BF),
            vmem((8, 128, 256), BF),
            vmem((512, 128), F32),
            vmem((40, 32, 128), BF),
            vmem((2, 16, 16, 1024), BF),
            vmem((256, 128), F32),
            vmem((8, 16, 512), BF),
            vmem((128, 128), F32),
            vmem((16, 1, 128), jnp.int32),
            smem((16, 1, 128), jnp.int32),
            smem((8, 32), jnp.int32),
            smem((1, 32), jnp.int32),
            smem((16, 32), jnp.int32),
            smem((1, 32), jnp.int32),
            smem((4, 16), jnp.int32),
            smem((1, 4), jnp.int32),
            dma((14,)),
            dma((16,)),
            dma((16,)),
            dma((8,)),
            dma((8,)),
            dma((16,)),
            dma((16,)),
            dma((16,)),
            dma((16,)),
            dma((2,)),
            dma((2,)),
            dma((4,)),
            dma((4,)),
        ],
        compiler_params=pltpu.CompilerParams(
            collective_id=0, has_side_effects=True, vmem_limit_bytes=63 * 1024 * 1024
        ),
        cost_estimate=pl.CostEstimate(
            flops=60_000_000, bytes_accessed=3_600_000, transcendentals=0
        ),
    )(
        points_in,
        leaf_basis,
        transfer,
        far_blocks,
        near_blocks,
        near_leaf.T,
        near_count.reshape(1, 32),
        far_slots.T,
        far_count.reshape(1, 32),
        recv_rows.reshape(1, 128),
        coarse_blocks,
        coarse_far,
        coarse_count.reshape(1, 4),
    )


def solution(mesh):
    in_specs = (
        P("grp", "leaf"),
        P(None, "leaf"),
        P("leaf", None),
        P("leaf", None, None),
        P("leaf", None, None),
        P("leaf", None),
        P("leaf"),
        P("leaf", None),
        P("leaf"),
        P("leaf", None, None),
        P("leaf", "grp", None),
        P("leaf", None),
        P("leaf"),
    )
    out_specs = P("grp", "leaf")
    return jax.shard_map(
        per_device, mesh=mesh, in_specs=in_specs, out_specs=out_specs, check_vma=False
    )
```

```python
import jax
import jax.numpy as jnp
from jax import lax
from jax.experimental import pallas as pl
from jax.experimental.pallas import tpu as pltpu
from jax.sharding import PartitionSpec as P

BF = jnp.bfloat16
F32 = jnp.float32
MESH = pl.DeviceIdType.MESH


def dot_nt(a, b):
    return lax.dot_general(a, b, (((1,), (1,)), ((), ())), preferred_element_type=F32)


def dot_nn(a, b):
    return jnp.dot(a, b, preferred_element_type=F32)


def iotas(shape):
    row = lax.broadcasted_iota(jnp.int32, shape, 0)
    col = lax.broadcasted_iota(jnp.int32, shape, 1)
    return row, col


def ones_where(cond):
    return jnp.where(cond, 1.0, 0.0).astype(BF)


def expand(tiles):
    _, col = iotas((8, 128))
    masks = [jnp.where((col >> 5) == r4, 1.0, 0.0) for r4 in range(4)]
    return jnp.concatenate([tile * mask for tile in tiles for mask in masks], axis=0).astype(BF)


def lane_tiles(value):
    return [value[:, 128 * t : 128 * t + 128] for t in range(value.shape[1] // 128)]


def diagonal(product, rows, entries):
    _, col = iotas((rows, product.shape[1]))
    kept = product[0:rows]
    for k in range(1, entries):
        kept = jnp.where((col & (entries - 1)) == k, product[rows * k : rows * k + rows], kept)
    return kept


def spread_matrix():
    row, col = iotas((128, 512))
    return ones_where(((row >> 5) == (col >> 7)) & ((row & 31) == (col & 31)))


def place_matrix(j):
    row, col = iotas((128, 512))
    return ones_where(((row >> 5) == (col >> 7)) & ((col & 127) == (j * 32 + (row & 31))))


def kernel(
    points_h,
    basis_h,
    transfer_h,
    far_h,
    near_h,
    near_leaf_h,
    near_count_h,
    far_slots_h,
    far_count_h,
    recv_h,
    coarse_h,
    coarse_far_h,
    coarse_count_h,
    out_ref,
    pts,
    bas,
    trn,
    farv,
    nearv,
    cb,
    halo,
    p1,
    rown,
    pw,
    tp,
    r2,
    send,
    fbuf,
    tt,
    wf,
    vf,
    bs,
    tn,
    nr,
    nf,
    dr,
    dn,
    idxv,
    idxs,
    nls,
    ncs,
    fss,
    fcs,
    cfs,
    ccs,
    load_sem,
    idx_ssem,
    idx_rsem,
    p1_ssem,
    p1_rsem,
    p2_ssem,
    p2_rsem,
    pw_ssem,
    pw_rsem,
    halo_ssem,
    halo_rsem,
    cb_ssem,
    cb_rsem,
):
    me = lax.axis_index("leaf")
    grp = lax.axis_index("grp")
    core = lax.rem(me, 2)
    y = lax.rem(lax.div(me, 2), 8)
    z = lax.div(me, 16)
    in_group = lax.rem(me, 16)
    place = (1 - core) * z + core * y
    line = (1 - core) * y + core * z
    own_server = core * 8 + line
    own_client = line * 2 + core

    def line_peer(o):
        turned = lax.rem(place + o, 8)
        return ((1 - core) * (turned * 16 + y * 2) + core * (z * 16 + turned * 2 + 1), grp)

    def server(m):
        kind, at = lax.div(m, 8), lax.rem(m, 8)
        return ((1 - kind) * (z * 16 + at * 2) + kind * (at * 16 + y * 2 + 1), grp)

    def client_slot(m):
        kind = lax.div(m, 8)
        return ((1 - kind) * y + kind * z) * 2 + core

    def client(slot):
        at, c = lax.div(slot, 2), lax.rem(slot, 2)
        return ((1 - core) * (z * 16 + at * 2) + core * (at * 16 + y * 2) + c, grp)

    def group_peer(o):
        return (z * 16 + lax.rem(in_group + o, 16), grp)

    def column_peer(o):
        turned = lax.rem(z + (o >> 1), 8)
        return (turned * 16 + y * 2 + lax.rem(core + (o & 1), 2), grp)

    up = (lax.rem(me + 1, 128), grp)
    down = (lax.rem(me + 127, 128), grp)

    def grp_peer(o):
        return (me, lax.rem(grp + o, 4))

    loads = {}

    def load(name, src, dst, n):
        loads[name] = pltpu.make_async_copy(src, dst, load_sem.at[n])
        loads[name].start()

    load("points", points_h, pts, 0)
    load("basis", basis_h, bas, 1)
    load("transfer", transfer_h, trn, 2)
    load("recv", recv_h, idxv.at[own_client], 3)
    load("coarse", coarse_h, cb.at[grp], 4)

    barrier = pltpu.get_barrier_semaphore()
    peers = [group_peer(o) for o in range(1, 16)]
    peers += [column_peer(o) for o in range(2, 16)]
    peers += [up, down]
    peers += [grp_peer(o) for o in range(1, 4)]
    for peer in peers:
        pl.semaphore_signal(barrier, inc=1, device_id=peer, device_id_type=MESH)

    load("near_leaf", near_leaf_h, nls, 5)
    load("near_count", near_count_h, ncs, 6)
    load("far_slots", far_slots_h, fss, 7)
    load("far_count", far_count_h, fcs, 8)
    load("coarse_far", coarse_far_h, cfs, 9)
    load("coarse_count", coarse_count_h, ccs, 10)
    load("far", far_h, farv, 12)
    load("near", near_h, nearv, 11)

    loads["points"].wait()
    loads["basis"].wait()
    _, col = iotas((32, 256))
    quad_masks = [ones_where((col >> 6) == l4) for l4 in range(4)]
    for quad in range(8):
        lanes = slice(256 * quad, 256 * quad + 256)
        v = bas[:, lanes]
        vv = jnp.concatenate([v * mask for mask in quad_masks], axis=0)
        p1[0, quad] = dot_nt(pts[:, lanes], vv).astype(BF)

    loads["recv"].wait()
    loads["coarse"].wait()
    def prepare(quad, _):
        sub, _ = iotas((16, 1024))
        for l4 in range(4):
            l = 4 * quad + l4
            blocks = jnp.where(sub < fcs[0, l], farv[l].astype(F32), 0.0)
            for t, tile in enumerate(lane_tiles(blocks)):
                bs[pl.ds((8 * l4 + t) * 16, 16), :] = tile
        _, col = iotas((32, 128))
        masks = [jnp.where((col >> 5) == r4, 1.0, 0.0) for r4 in range(4)]
        row, col = iotas((32, 128))
        gather = ones_where((col & 31) == row)
        for k in range(16):
            tile = bs[pl.ds(k, 32, stride=16), :]
            rows = jnp.concatenate([tile * mask for mask in masks], axis=0).astype(BF)
            wf[quad, 32 * k : 32 * k + 32, :] = dot_nt(gather, rows).astype(BF)
        return 0

    def prepare_all():
        loads["far"].wait()
        loads["far_count"].wait()
        lax.fori_loop(0, 8, prepare, 0)
        row, col = iotas((128, 32))
        permute = ones_where(col == 4 * (row & 7) + (row >> 5))
        row, col = iotas((128, 256))
        block = ((row >> 3) & 3) == (col >> 6)
        for quad in range(8):
            rows = dot_nn(permute, bas[:, 256 * quad : 256 * quad + 256])
            vf[quad] = jnp.where(block, rows, 0.0).astype(BF)

    _, col = iotas((16, 128))
    left = jnp.where(col < 64, 1.0, 0.0)
    right = 1.0 - left

    def near_table(m, tile):
        value = tile.astype(F32)
        turned = pltpu.roll(value, 64, 1)
        tn[m] = jnp.concatenate([value * left, turned * right], axis=0).astype(BF)
        tn[m + 1] = jnp.concatenate([turned * left, value * right], axis=0).astype(BF)

    def near_pair(j, _):
        _, lane = iotas((32, 256))
        for l2 in range(2):
            l = 2 * j + l2
            blocks = nearv[l].astype(F32)
            flat = jnp.concatenate(lane_tiles(blocks), axis=0).astype(BF)
            source = jnp.concatenate(
                [tn[jnp.clip(nls[k, l] - me * 32 + 4, 0, 39)] for k in range(8)], axis=0
            )
            kept = diagonal(dot_nt(source, flat), 32, 8)
            kept = jnp.where((lane & 7) < ncs[0, l], kept, 0.0)
            high = kept.astype(BF)
            for part, value in enumerate([high, (kept - high.astype(F32)).astype(BF)]):
                nr[part, j, :, 512 * l2 : 512 * l2 + 256] = value[0:16]
                nr[part, j, :, 512 * l2 + 256 : 512 * l2 + 512] = value[16:32]
        return 0

    def inner_work():
        prepare_all()
        for j in range(16):
            near_table(4 + 2 * j, pts[:, 128 * j : 128 * j + 128])
        loads["near"].wait()
        loads["near_leaf"].wait()
        loads["near_count"].wait()
        lax.fori_loop(2, 14, near_pair, 0)

    @pl.when(z < 4)
    def _():
        inner_work()

    pl.semaphore_wait(barrier, len(peers))

    sends = []

    def remote(src, dst, ssem, rsem, peer):
        copy = pltpu.make_async_remote_copy(
            src_ref=src,
            dst_ref=dst,
            send_sem=ssem,
            recv_sem=rsem,
            device_id=peer,
            device_id_type=MESH,
        )
        copy.start()
        sends.append(copy)
        return copy

    p1_copies = {
        8 - o: remote(
            p1.at[0],
            p1.at[8 - o],
            p1_ssem.at[o],
            p1_rsem.at[8 - o],
            line_peer(o),
        )
        for o in (4, 3, 5, 2, 6, 1, 7)
    }
    idx_copies = []
    for o in range(1, 16):
        m = lax.rem(own_server + o, 16)
        slot = client_slot(m)
        idx_copies.append(
            remote(
                idxv.at[own_client],
                idxv.at[slot],
                idx_ssem.at[o],
                idx_rsem.at[slot],
                server(m),
            )
        )
    halo_copies = [
        remote(pts.at[:, pl.ds(1792, 256)], halo.at[0], halo_ssem.at[0], halo_rsem.at[0], up),
        remote(pts.at[:, pl.ds(0, 256)], halo.at[1], halo_ssem.at[1], halo_rsem.at[1], down),
    ]
    cb_copies = [
        remote(cb.at[grp], cb.at[grp], cb_ssem.at[o], cb_rsem.at[o], grp_peer(o))
        for o in range(1, 4)
    ]

    spread = spread_matrix()
    wide = dot_nn(p1[0].reshape(128, 128), spread).astype(BF)
    for quad in range(8):
        for a in range(4):
            rown[4 * quad + a] = wide[16 * quad : 16 * quad + 16, 128 * a : 128 * a + 128]
    loads["transfer"].wait()
    total = jnp.zeros((16, 128), F32)
    row, col = iotas((256, 128))
    for c in range(4):
        ex = expand(lane_tiles(trn[8 * c : 8 * c + 8, :].astype(F32)))
        product = dot_nt(rown[8 * c : 8 * c + 8].reshape(128, 128), ex)
        kept = diagonal(product, 16, 8).astype(BF)
        total += dot_nn(kept, ones_where(col == c * 32 + (row >> 3)))
    pw[in_group] = total.astype(BF)

    pw_copies = [
        remote(pw.at[in_group], pw.at[in_group], pw_ssem.at[o], pw_rsem.at[o], group_peer(o))
        for o in range(1, 16)
    ]

    for o in range(1, 16):
        slot = lax.rem(own_client + o, 16)
        pltpu.make_async_copy(idxv.at[slot], idxv.at[slot], idx_rsem.at[slot]).wait()
    to_smem = pltpu.make_async_copy(idxv, idxs, load_sem.at[13])
    to_smem.start()
    for batch in (range(0, 4), range(4, 8)):
        for i in batch:
            if i:
                p1_copies[i].wait_recv()
        for i in batch:
            wide = dot_nn(p1[i].reshape(128, 128), place_matrix(i % 4)).astype(BF)
            for quad in range(8):
                for a in range(4):
                    r2[32 * i + 4 * quad + a] = wide[
                        16 * quad : 16 * quad + 16, 128 * a : 128 * a + 128
                    ]
    to_smem.wait()
    owners = []
    for i in range(8):
        turned = lax.rem(place + i, 8)
        owners.append((1 - core) * (turned * 16 + y * 2) + core * (z * 16 + turned * 2 + 1))
    p2_copies = []
    for o in (8, 9, 7, 10, 6, 11, 5, 12, 4, 13, 3, 14, 2, 15, 1, 0):
        slot = lax.rem(own_client + o, 16)
        for g in range(2):
            tile = r2[32 * (4 * g) + idxs[slot, 0, owners[4 * g]]]
            for j in range(1, 4):
                m = 4 * g + j
                tile = tile + r2[32 * m + idxs[slot, 0, owners[m]]]
            if o == 0:
                fbuf[own_server, g] = tile
            else:
                send[o, g] = tile
        if o:
            p2_copies.append(
                remote(
                    send.at[o],
                    fbuf.at[own_server],
                    p2_ssem.at[o],
                    p2_rsem.at[own_server],
                    client(slot),
                )
            )

    @pl.when(z >= 4)
    def _():
        inner_work()

    for copy in halo_copies:
        copy.wait_recv()
    for j in range(2):
        near_table(2 * j, halo[0, :, 128 * j : 128 * j + 128])
        near_table(36 + 2 * j, halo[1, :, 128 * j : 128 * j + 128])
    lax.fori_loop(0, 2, near_pair, 0)
    lax.fori_loop(14, 16, near_pair, 0)
    row, col = iotas((1024, 128))
    group = row >> 8
    fold_near = ones_where(col == (group >> 1) * 64 + ((row & 255) >> 3) * 2 + (group & 1))
    nf[...] = dot_nn(nr[0].reshape(256, 1024), fold_near)
    nf[...] += dot_nn(nr[1].reshape(256, 1024), fold_near)

    for copy in pw_copies:
        copy.wait_recv()
    wide = dot_nn(pw[...].reshape(256, 128), spread).astype(BF)
    for device in range(16):
        for c in range(4):
            tp[4 * device + c] = wide[16 * device : 16 * device + 16, 128 * c : 128 * c + 128]
    for copy in cb_copies:
        copy.wait_recv()
    loads["coarse_far"].wait()
    loads["coarse_count"].wait()
    total = jnp.zeros((16, 128), F32)
    sub, _ = iotas((8, 1024))
    row, col = iotas((256, 128))
    for cp in range(2):
        counts = jnp.where(sub < 4, ccs[0, 2 * cp], ccs[0, 2 * cp + 1])
        product = jnp.zeros((128, 256), F32)
        for gp in range(2):
            halves = []
            for g in (2 * gp, 2 * gp + 1):
                rows = jnp.concatenate(
                    [cb[g, 2 * cp].astype(F32), cb[g, 2 * cp + 1].astype(F32)], axis=0
                )
                rows = jnp.where((sub & 3) + 4 * g < counts, rows, 0.0)
                halves.append(expand(lane_tiles(rows)))
            weights = jnp.concatenate(halves, axis=1)
            source = jnp.concatenate(
                [
                    jnp.concatenate(
                        [
                            tp[cfs[2 * cp + (k >> 2), 4 * g + (k & 3)] & 63]
                            for g in (2 * gp, 2 * gp + 1)
                        ],
                        axis=1,
                    )
                    for k in range(8)
                ],
                axis=0,
            )
            product += dot_nt(source, weights)
        kept = diagonal(product, 16, 8).astype(BF)
        target = (2 * cp + ((row & 7) >> 2)) * 32 + (row >> 3)
        total += dot_nn(kept, ones_where(col == target))
    field = total.astype(BF)

    row, col = iotas((128, 256))
    flat = jnp.concatenate(lane_tiles(trn[...]), axis=0)
    spreads = []
    for r4 in range(4):
        hit = ((row >> 5) == ((col & 31) >> 3)) & (((row & 31) >> 2) == (col >> 5))
        spreads.append(dot_nn(field, ones_where(hit & ((row & 3) == r4))).astype(BF))
    _, lane = iotas((16, 256))
    _, col = iotas((16, 128))
    for part in range(4):
        pieces = []
        for l in range(8 * part, 8 * part + 8):
            mask = ones_where((lane & 31) == l)
            pieces += [spreads[r4] * mask for r4 in range(4)]
        product = dot_nn(jnp.concatenate(pieces, axis=0), flat)
        for i in range(8):
            kept = product[64 * i : 64 * i + 16]
            for r4 in range(1, 4):
                at = 64 * i + 16 * r4
                kept = jnp.where((col >> 5) == r4, product[at : at + 16], kept)
            l = 8 * part + i
            dr[l // 4, :, 128 * (l % 4) : 128 * (l % 4) + 128] = kept.astype(BF)
    row, col = iotas((512, 128))
    hit = ((row >> 7) == ((col >> 3) & 3)) & ((row & 31) == 4 * (col & 7) + (col >> 5))
    dn[...] = dot_nn(dr[...].reshape(128, 512), ones_where(hit))

    loads["far_slots"].wait()
    for o in range(1, 16):
        m = lax.rem(own_server + o, 16)
        pltpu.make_async_copy(fbuf.at[m], fbuf.at[m], p2_rsem.at[m]).wait()
    wide = dot_nn(fbuf[...].reshape(512, 128), spread).astype(BF)
    for m in range(16):
        for i in range(8):
            row_owner = lax.rem(z + i, 8) * 16 + 2 * m
            column_owner = (m - 8) * 16 + lax.rem(y + i, 8) * 2 + 1
            f = row_owner if m < 8 else column_owner
            row, lane = 32 * m + 16 * (i // 4), 128 * (i % 4)
            tt[f] = wide[row : row + 16, lane : lane + 128]
    _, col = iotas((16, 128))
    parts = [ones_where((col >> 5) == j) for j in range(4)]
    for quad in range(8):
        rows = []
        for l in range(4 * quad, 4 * quad + 4):
            tiles = []
            for k in range(0, 16, 4):
                tile = tt[fss[k, l]] * parts[0]
                for j in range(1, 4):
                    tile = tile + tt[fss[k + j, l]] * parts[j]
                tiles.append(tile)
            rows.append(jnp.concatenate(tiles, axis=1))
        product = dot_nn(jnp.concatenate(rows, axis=0), wf[quad])
        local = product[0:16]
        for l4 in range(1, 4):
            local = jnp.where(((col >> 3) & 3) == l4, product[16 * l4 : 16 * l4 + 16], local)
        local = (local + dn[16 * quad : 16 * quad + 16]).astype(BF)
        near = jnp.concatenate(
            [nf[32 * quad : 32 * quad + 16], nf[32 * quad + 16 : 32 * quad + 32]], axis=1
        )
        out_ref[:, 256 * quad : 256 * quad + 256] = (dot_nn(local, vf[quad]) + near).astype(BF)

    for copy in sends:
        copy.wait_send()


def per_device(
    points_in,
    leaf_basis,
    transfer,
    far_blocks,
    near_blocks,
    near_leaf,
    near_count,
    far_slots,
    far_count,
    recv_rows,
    coarse_blocks,
    coarse_far,
    coarse_count,
):
    vmem = pltpu.VMEM
    smem = pltpu.SMEM
    dma = pltpu.SemaphoreType.DMA
    anywhere = pl.BlockSpec(memory_space=pltpu.HBM)
    return pl.pallas_call(
        kernel,
        out_shape=jax.ShapeDtypeStruct((16, 2048), BF),
        in_specs=[anywhere] * 13,
        out_specs=pl.BlockSpec(memory_space=pltpu.VMEM),
        scratch_shapes=[
            vmem((16, 2048), BF),
            vmem((32, 2048), BF),
            vmem((32, 1024), BF),
            vmem((32, 16, 1024), BF),
            vmem((32, 8, 4096), BF),
            vmem((4, 4, 4, 1024), BF),
            vmem((2, 16, 256), BF),
            vmem((8, 8, 16, 128), BF),
            vmem((32, 16, 128), BF),
            vmem((16, 16, 128), BF),
            vmem((64, 16, 128), BF),
            vmem((256, 16, 128), BF),
            vmem((16, 2, 16, 128), BF),
            vmem((16, 2, 16, 128), BF),
            vmem((128, 16, 128), BF),
            vmem((8, 512, 128), BF),
            vmem((8, 128, 256), BF),
            vmem((512, 128), F32),
            vmem((40, 32, 128), BF),
            vmem((2, 16, 16, 1024), BF),
            vmem((256, 128), F32),
            vmem((8, 16, 512), BF),
            vmem((128, 128), F32),
            vmem((16, 1, 128), jnp.int32),
            smem((16, 1, 128), jnp.int32),
            smem((8, 32), jnp.int32),
            smem((1, 32), jnp.int32),
            smem((16, 32), jnp.int32),
            smem((1, 32), jnp.int32),
            smem((4, 16), jnp.int32),
            smem((1, 4), jnp.int32),
            dma((14,)),
            dma((16,)),
            dma((16,)),
            dma((8,)),
            dma((8,)),
            dma((16,)),
            dma((16,)),
            dma((16,)),
            dma((16,)),
            dma((2,)),
            dma((2,)),
            dma((4,)),
            dma((4,)),
        ],
        compiler_params=pltpu.CompilerParams(
            collective_id=0, has_side_effects=True, vmem_limit_bytes=63 * 1024 * 1024
        ),
        cost_estimate=pl.CostEstimate(
            flops=60_000_000, bytes_accessed=3_600_000, transcendentals=0
        ),
    )(
        points_in,
        leaf_basis,
        transfer,
        far_blocks,
        near_blocks,
        near_leaf.T,
        near_count.reshape(1, 32),
        far_slots.T,
        far_count.reshape(1, 32),
        recv_rows.reshape(1, 128),
        coarse_blocks,
        coarse_far,
        coarse_count.reshape(1, 4),
    )


def solution(mesh):
    in_specs = (
        P("grp", "leaf"),
        P(None, "leaf"),
        P("leaf", None),
        P("leaf", None, None),
        P("leaf", None, None),
        P("leaf", None),
        P("leaf"),
        P("leaf", None),
        P("leaf"),
        P("leaf", None, None),
        P("leaf", "grp", None),
        P("leaf", None),
        P("leaf"),
    )
    out_specs = P("grp", "leaf")
    return jax.shard_map(
        per_device, mesh=mesh, in_specs=in_specs, out_specs=out_specs, check_vma=False
    )
```

```python
import jax
import jax.numpy as jnp
from jax import lax
from jax.experimental import pallas as pl
from jax.experimental.pallas import tpu as pltpu
from jax.sharding import PartitionSpec as P

BF = jnp.bfloat16
F32 = jnp.float32
MESH = pl.DeviceIdType.MESH


def dot_nt(a, b):
    return lax.dot_general(a, b, (((1,), (1,)), ((), ())), preferred_element_type=F32)


def dot_nn(a, b):
    return jnp.dot(a, b, preferred_element_type=F32)


def iotas(shape):
    row = lax.broadcasted_iota(jnp.int32, shape, 0)
    col = lax.broadcasted_iota(jnp.int32, shape, 1)
    return row, col


def ones_where(cond):
    return jnp.where(cond, 1.0, 0.0).astype(BF)


def expand(tiles):
    _, col = iotas((8, 128))
    masks = [jnp.where((col >> 5) == r4, 1.0, 0.0) for r4 in range(4)]
    return jnp.concatenate([tile * mask for tile in tiles for mask in masks], axis=0).astype(BF)


def lane_tiles(value):
    return [value[:, 128 * t : 128 * t + 128] for t in range(value.shape[1] // 128)]


def diagonal(product, rows, entries):
    _, col = iotas((rows, product.shape[1]))
    kept = product[0:rows]
    for k in range(1, entries):
        kept = jnp.where((col & (entries - 1)) == k, product[rows * k : rows * k + rows], kept)
    return kept


def spread_matrix():
    row, col = iotas((128, 512))
    return ones_where(((row >> 5) == (col >> 7)) & ((row & 31) == (col & 31)))


def place_matrix(j):
    row, col = iotas((128, 512))
    return ones_where(((row >> 5) == (col >> 7)) & ((col & 127) == (j * 32 + (row & 31))))


def kernel(
    points_h,
    basis_h,
    transfer_h,
    far_h,
    near_h,
    near_leaf_h,
    near_count_h,
    far_slots_h,
    far_count_h,
    recv_h,
    coarse_h,
    coarse_far_h,
    coarse_count_h,
    out_ref,
    pts,
    bas,
    trn,
    farv,
    nearv,
    cb,
    halo,
    p1,
    rown,
    pw,
    tp,
    r2,
    send,
    fbuf,
    tt,
    wf,
    vf,
    bs,
    tn,
    nr,
    nf,
    dr,
    dn,
    idxv,
    idxs,
    nls,
    ncs,
    fss,
    fcs,
    cfs,
    ccs,
    load_sem,
    idx_ssem,
    idx_rsem,
    p1_ssem,
    p1_rsem,
    p2_ssem,
    p2_rsem,
    pw_ssem,
    pw_rsem,
    halo_ssem,
    halo_rsem,
    cb_ssem,
    cb_rsem,
):
    me = lax.axis_index("leaf")
    grp = lax.axis_index("grp")
    core = lax.rem(me, 2)
    y = lax.rem(lax.div(me, 2), 8)
    z = lax.div(me, 16)
    in_group = lax.rem(me, 16)
    place = (1 - core) * z + core * y
    line = (1 - core) * y + core * z
    own_server = core * 8 + line
    own_client = line * 2 + core

    def line_peer(o):
        turned = lax.rem(place + o, 8)
        return ((1 - core) * (turned * 16 + y * 2) + core * (z * 16 + turned * 2 + 1), grp)

    def server(m):
        kind, at = lax.div(m, 8), lax.rem(m, 8)
        return ((1 - kind) * (z * 16 + at * 2) + kind * (at * 16 + y * 2 + 1), grp)

    def client_slot(m):
        kind = lax.div(m, 8)
        return ((1 - kind) * y + kind * z) * 2 + core

    def client(slot):
        at, c = lax.div(slot, 2), lax.rem(slot, 2)
        return ((1 - core) * (z * 16 + at * 2) + core * (at * 16 + y * 2) + c, grp)

    def group_peer(o):
        return (z * 16 + lax.rem(in_group + o, 16), grp)

    def column_peer(o):
        turned = lax.rem(z + (o >> 1), 8)
        return (turned * 16 + y * 2 + lax.rem(core + (o & 1), 2), grp)

    up = (lax.rem(me + 1, 128), grp)
    down = (lax.rem(me + 127, 128), grp)

    def grp_peer(o):
        return (me, lax.rem(grp + o, 4))

    loads = {}

    def load(name, src, dst, n):
        loads[name] = pltpu.make_async_copy(src, dst, load_sem.at[n])
        loads[name].start()

    load("points", points_h, pts, 0)
    load("basis", basis_h, bas, 1)
    load("transfer", transfer_h, trn, 2)
    load("recv", recv_h, idxv.at[own_client], 3)
    load("coarse", coarse_h, cb.at[grp], 4)

    barrier = pltpu.get_barrier_semaphore()
    peers = [group_peer(o) for o in range(1, 16)]
    peers += [column_peer(o) for o in range(2, 16)]
    peers += [up, down]
    peers += [grp_peer(o) for o in range(1, 4)]
    for peer in peers:
        pl.semaphore_signal(barrier, inc=1, device_id=peer, device_id_type=MESH)

    load("near_leaf", near_leaf_h, nls, 5)
    load("near_count", near_count_h, ncs, 6)
    load("far_slots", far_slots_h, fss, 7)
    load("far_count", far_count_h, fcs, 8)
    load("coarse_far", coarse_far_h, cfs, 9)
    load("coarse_count", coarse_count_h, ccs, 10)
    load("far", far_h, farv, 12)
    load("near", near_h, nearv, 11)

    loads["points"].wait()
    loads["basis"].wait()
    _, col = iotas((32, 256))
    quad_masks = [ones_where((col >> 6) == l4) for l4 in range(4)]
    for quad in range(8):
        lanes = slice(256 * quad, 256 * quad + 256)
        v = bas[:, lanes]
        vv = jnp.concatenate([v * mask for mask in quad_masks], axis=0)
        p1[0, quad] = dot_nt(pts[:, lanes], vv).astype(BF)

    loads["recv"].wait()
    loads["coarse"].wait()
    def prepare(quad, _):
        sub, _ = iotas((16, 1024))
        for l4 in range(4):
            l = 4 * quad + l4
            blocks = jnp.where(sub < fcs[0, l], farv[l].astype(F32), 0.0)
            for t, tile in enumerate(lane_tiles(blocks)):
                bs[pl.ds((8 * l4 + t) * 16, 16), :] = tile
        _, col = iotas((32, 128))
        masks = [jnp.where((col >> 5) == r4, 1.0, 0.0) for r4 in range(4)]
        row, col = iotas((32, 128))
        gather = ones_where((col & 31) == row)
        for k in range(16):
            tile = bs[pl.ds(k, 32, stride=16), :]
            rows = jnp.concatenate([tile * mask for mask in masks], axis=0).astype(BF)
            wf[quad, 32 * k : 32 * k + 32, :] = dot_nt(gather, rows).astype(BF)
        return 0

    def prepare_all():
        loads["far"].wait()
        loads["far_count"].wait()
        lax.fori_loop(0, 8, prepare, 0)
        row, col = iotas((128, 32))
        permute = ones_where(col == 4 * (row & 7) + (row >> 5))
        row, col = iotas((128, 256))
        block = ((row >> 3) & 3) == (col >> 6)
        for quad in range(8):
            rows = dot_nn(permute, bas[:, 256 * quad : 256 * quad + 256])
            vf[quad] = jnp.where(block, rows, 0.0).astype(BF)

    _, col = iotas((16, 128))
    left = jnp.where(col < 64, 1.0, 0.0)
    right = 1.0 - left

    def near_table(m, tile):
        value = tile.astype(F32)
        turned = pltpu.roll(value, 64, 1)
        tn[m] = jnp.concatenate([value * left, turned * right], axis=0).astype(BF)
        tn[m + 1] = jnp.concatenate([turned * left, value * right], axis=0).astype(BF)

    def near_pair(j, _):
        _, lane = iotas((32, 256))
        for l2 in range(2):
            l = 2 * j + l2
            blocks = nearv[l].astype(F32)
            flat = jnp.concatenate(lane_tiles(blocks), axis=0).astype(BF)
            source = jnp.concatenate(
                [tn[jnp.clip(nls[k, l] - me * 32 + 4, 0, 39)] for k in range(8)], axis=0
            )
            kept = diagonal(dot_nt(source, flat), 32, 8)
            kept = jnp.where((lane & 7) < ncs[0, l], kept, 0.0)
            high = kept.astype(BF)
            for part, value in enumerate([high, (kept - high.astype(F32)).astype(BF)]):
                nr[part, j, :, 512 * l2 : 512 * l2 + 256] = value[0:16]
                nr[part, j, :, 512 * l2 + 256 : 512 * l2 + 512] = value[16:32]
        return 0

    def inner_work():
        prepare_all()
        for j in range(16):
            near_table(4 + 2 * j, pts[:, 128 * j : 128 * j + 128])
        loads["near"].wait()
        loads["near_leaf"].wait()
        loads["near_count"].wait()
        lax.fori_loop(2, 14, near_pair, 0)

    @pl.when(z < 4)
    def _():
        inner_work()

    pl.semaphore_wait(barrier, len(peers))

    sends = []

    def remote(src, dst, ssem, rsem, peer):
        copy = pltpu.make_async_remote_copy(
            src_ref=src,
            dst_ref=dst,
            send_sem=ssem,
            recv_sem=rsem,
            device_id=peer,
            device_id_type=MESH,
        )
        copy.start()
        sends.append(copy)
        return copy

    p1_copies = {
        8 - o: remote(
            p1.at[0],
            p1.at[8 - o],
            p1_ssem.at[o],
            p1_rsem.at[8 - o],
            line_peer(o),
        )
        for o in (4, 3, 5, 2, 6, 1, 7)
    }
    idx_copies = []
    for o in range(1, 16):
        m = lax.rem(own_server + o, 16)
        slot = client_slot(m)
        idx_copies.append(
            remote(
                idxv.at[own_client],
                idxv.at[slot],
                idx_ssem.at[o],
                idx_rsem.at[slot],
                server(m),
            )
        )
    halo_copies = [
        remote(pts.at[:, pl.ds(1792, 256)], halo.at[0], halo_ssem.at[0], halo_rsem.at[0], up),
        remote(pts.at[:, pl.ds(0, 256)], halo.at[1], halo_ssem.at[1], halo_rsem.at[1], down),
    ]
    cb_copies = [
        remote(cb.at[grp], cb.at[grp], cb_ssem.at[o], cb_rsem.at[o], grp_peer(o))
        for o in range(1, 4)
    ]

    spread = spread_matrix()
    wide = dot_nn(p1[0].reshape(128, 128), spread).astype(BF)
    for quad in range(8):
        for a in range(4):
            rown[4 * quad + a] = wide[16 * quad : 16 * quad + 16, 128 * a : 128 * a + 128]
    loads["transfer"].wait()
    total = jnp.zeros((16, 128), F32)
    row, col = iotas((256, 128))
    for c in range(4):
        ex = expand(lane_tiles(trn[8 * c : 8 * c + 8, :].astype(F32)))
        product = dot_nt(rown[8 * c : 8 * c + 8].reshape(128, 128), ex)
        kept = diagonal(product, 16, 8).astype(BF)
        total += dot_nn(kept, ones_where(col == c * 32 + (row >> 3)))
    pw[in_group] = total.astype(BF)

    pw_copies = [
        remote(pw.at[in_group], pw.at[in_group], pw_ssem.at[o], pw_rsem.at[o], group_peer(o))
        for o in range(1, 16)
    ]

    for o in range(1, 16):
        slot = lax.rem(own_client + o, 16)
        pltpu.make_async_copy(idxv.at[slot], idxv.at[slot], idx_rsem.at[slot]).wait()
    to_smem = pltpu.make_async_copy(idxv, idxs, load_sem.at[13])
    to_smem.start()
    for batch in (range(0, 4), range(4, 8)):
        for i in batch:
            if i:
                p1_copies[i].wait_recv()
        for i in batch:
            wide = dot_nn(p1[i].reshape(128, 128), place_matrix(i % 4)).astype(BF)
            for quad in range(8):
                for a in range(4):
                    r2[32 * i + 4 * quad + a] = wide[
                        16 * quad : 16 * quad + 16, 128 * a : 128 * a + 128
                    ]
    to_smem.wait()
    owners = []
    for i in range(8):
        turned = lax.rem(place + i, 8)
        owners.append((1 - core) * (turned * 16 + y * 2) + core * (z * 16 + turned * 2 + 1))
    p2_copies = []
    for o in (8, 9, 7, 10, 6, 11, 5, 12, 4, 13, 3, 14, 2, 15, 1, 0):
        slot = lax.rem(own_client + o, 16)
        for g in range(2):
            tile = r2[32 * (4 * g) + idxs[slot, 0, owners[4 * g]]]
            for j in range(1, 4):
                m = 4 * g + j
                tile = tile + r2[32 * m + idxs[slot, 0, owners[m]]]
            if o == 0:
                fbuf[own_server, g] = tile
            else:
                send[o, g] = tile
        if o:
            p2_copies.append(
                remote(
                    send.at[o],
                    fbuf.at[own_server],
                    p2_ssem.at[o],
                    p2_rsem.at[own_server],
                    client(slot),
                )
            )

    @pl.when(z >= 4)
    def _():
        inner_work()

    for copy in halo_copies:
        copy.wait_recv()
    for j in range(2):
        near_table(2 * j, halo[0, :, 128 * j : 128 * j + 128])
        near_table(36 + 2 * j, halo[1, :, 128 * j : 128 * j + 128])
    lax.fori_loop(0, 2, near_pair, 0)
    lax.fori_loop(14, 16, near_pair, 0)
    row, col = iotas((1024, 128))
    group = row >> 8
    fold_near = ones_where(col == (group >> 1) * 64 + ((row & 255) >> 3) * 2 + (group & 1))
    nf[...] = dot_nn(nr[0].reshape(256, 1024), fold_near)
    nf[...] += dot_nn(nr[1].reshape(256, 1024), fold_near)

    for copy in pw_copies:
        copy.wait_recv()
    wide = dot_nn(pw[...].reshape(256, 128), spread).astype(BF)
    for device in range(16):
        for c in range(4):
            tp[4 * device + c] = wide[16 * device : 16 * device + 16, 128 * c : 128 * c + 128]
    for copy in cb_copies:
        copy.wait_recv()
    loads["coarse_far"].wait()
    loads["coarse_count"].wait()
    total = jnp.zeros((16, 128), F32)
    sub, _ = iotas((8, 1024))
    row, col = iotas((256, 128))
    for cp in range(2):
        counts = jnp.where(sub < 4, ccs[0, 2 * cp], ccs[0, 2 * cp + 1])
        product = jnp.zeros((128, 256), F32)
        for gp in range(2):
            halves = []
            for g in (2 * gp, 2 * gp + 1):
                rows = jnp.concatenate(
                    [cb[g, 2 * cp].astype(F32), cb[g, 2 * cp + 1].astype(F32)], axis=0
                )
                rows = jnp.where((sub & 3) + 4 * g < counts, rows, 0.0)
                halves.append(expand(lane_tiles(rows)))
            weights = jnp.concatenate(halves, axis=1)
            source = jnp.concatenate(
                [
                    jnp.concatenate(
                        [
                            tp[cfs[2 * cp + (k >> 2), 4 * g + (k & 3)] & 63]
                            for g in (2 * gp, 2 * gp + 1)
                        ],
                        axis=1,
                    )
                    for k in range(8)
                ],
                axis=0,
            )
            product += dot_nt(source, weights)
        kept = diagonal(product, 16, 8).astype(BF)
        target = (2 * cp + ((row & 7) >> 2)) * 32 + (row >> 3)
        total += dot_nn(kept, ones_where(col == target))
    field = total.astype(BF)

    row, col = iotas((128, 256))
    flat = jnp.concatenate(lane_tiles(trn[...]), axis=0)
    spreads = []
    for r4 in range(4):
        hit = ((row >> 5) == ((col & 31) >> 3)) & (((row & 31) >> 2) == (col >> 5))
        spreads.append(dot_nn(field, ones_where(hit & ((row & 3) == r4))).astype(BF))
    _, lane = iotas((16, 256))
    _, col = iotas((16, 128))
    for part in range(4):
        pieces = []
        for l in range(8 * part, 8 * part + 8):
            mask = ones_where((lane & 31) == l)
            pieces += [spreads[r4] * mask for r4 in range(4)]
        product = dot_nn(jnp.concatenate(pieces, axis=0), flat)
        for i in range(8):
            kept = product[64 * i : 64 * i + 16]
            for r4 in range(1, 4):
                at = 64 * i + 16 * r4
                kept = jnp.where((col >> 5) == r4, product[at : at + 16], kept)
            l = 8 * part + i
            dr[l // 4, :, 128 * (l % 4) : 128 * (l % 4) + 128] = kept.astype(BF)
    row, col = iotas((512, 128))
    hit = ((row >> 7) == ((col >> 3) & 3)) & ((row & 31) == 4 * (col & 7) + (col >> 5))
    dn[...] = dot_nn(dr[...].reshape(128, 512), ones_where(hit))

    loads["far_slots"].wait()
    for o in range(1, 16):
        m = lax.rem(own_server + o, 16)
        pltpu.make_async_copy(fbuf.at[m], fbuf.at[m], p2_rsem.at[m]).wait()
    wide = dot_nn(fbuf[...].reshape(512, 128), spread).astype(BF)
    for m in range(16):
        for i in range(8):
            row_owner = lax.rem(z + i, 8) * 16 + 2 * m
            column_owner = (m - 8) * 16 + lax.rem(y + i, 8) * 2 + 1
            f = row_owner if m < 8 else column_owner
            row, lane = 32 * m + 16 * (i // 4), 128 * (i % 4)
            tt[f] = wide[row : row + 16, lane : lane + 128]
    _, col = iotas((16, 128))
    parts = [ones_where((col >> 5) == j) for j in range(4)]
    for quad in range(8):
        rows = []
        for l in range(4 * quad, 4 * quad + 4):
            tiles = []
            for k in range(0, 16, 4):
                tile = tt[fss[k, l]] * parts[0]
                for j in range(1, 4):
                    tile = tile + tt[fss[k + j, l]] * parts[j]
                tiles.append(tile)
            rows.append(jnp.concatenate(tiles, axis=1))
        product = dot_nn(jnp.concatenate(rows, axis=0), wf[quad])
        local = product[0:16]
        for l4 in range(1, 4):
            local = jnp.where(((col >> 3) & 3) == l4, product[16 * l4 : 16 * l4 + 16], local)
        local = (local + dn[16 * quad : 16 * quad + 16]).astype(BF)
        near = jnp.concatenate(
            [nf[32 * quad : 32 * quad + 16], nf[32 * quad + 16 : 32 * quad + 32]], axis=1
        )
        out_ref[:, 256 * quad : 256 * quad + 256] = (dot_nn(local, vf[quad]) + near).astype(BF)

    for copy in sends:
        copy.wait_send()


def per_device(
    points_in,
    leaf_basis,
    transfer,
    far_blocks,
    near_blocks,
    near_leaf,
    near_count,
    far_slots,
    far_count,
    recv_rows,
    coarse_blocks,
    coarse_far,
    coarse_count,
):
    vmem = pltpu.VMEM
    smem = pltpu.SMEM
    dma = pltpu.SemaphoreType.DMA
    anywhere = pl.BlockSpec(memory_space=pltpu.HBM)
    return pl.pallas_call(
        kernel,
        out_shape=jax.ShapeDtypeStruct((16, 2048), BF),
        in_specs=[anywhere] * 13,
        out_specs=pl.BlockSpec(memory_space=pltpu.VMEM),
        scratch_shapes=[
            vmem((16, 2048), BF),
            vmem((32, 2048), BF),
            vmem((32, 1024), BF),
            vmem((32, 16, 1024), BF),
            vmem((32, 8, 4096), BF),
            vmem((4, 4, 4, 1024), BF),
            vmem((2, 16, 256), BF),
            vmem((8, 8, 16, 128), BF),
            vmem((32, 16, 128), BF),
            vmem((16, 16, 128), BF),
            vmem((64, 16, 128), BF),
            vmem((256, 16, 128), BF),
            vmem((16, 2, 16, 128), BF),
            vmem((16, 2, 16, 128), BF),
            vmem((128, 16, 128), BF),
            vmem((8, 512, 128), BF),
            vmem((8, 128, 256), BF),
            vmem((528, 128), F32),
            vmem((40, 32, 128), BF),
            vmem((2, 16, 16, 1024), BF),
            vmem((256, 128), F32),
            vmem((8, 16, 512), BF),
            vmem((128, 128), F32),
            vmem((16, 1, 128), jnp.int32),
            smem((16, 1, 128), jnp.int32),
            smem((8, 32), jnp.int32),
            smem((1, 32), jnp.int32),
            smem((16, 32), jnp.int32),
            smem((1, 32), jnp.int32),
            smem((4, 16), jnp.int32),
            smem((1, 4), jnp.int32),
            dma((14,)),
            dma((16,)),
            dma((16,)),
            dma((8,)),
            dma((8,)),
            dma((16,)),
            dma((16,)),
            dma((16,)),
            dma((16,)),
            dma((2,)),
            dma((2,)),
            dma((4,)),
            dma((4,)),
        ],
        compiler_params=pltpu.CompilerParams(
            collective_id=0, has_side_effects=True, vmem_limit_bytes=63 * 1024 * 1024
        ),
        cost_estimate=pl.CostEstimate(
            flops=60_000_000, bytes_accessed=3_600_000, transcendentals=0
        ),
    )(
        points_in,
        leaf_basis,
        transfer,
        far_blocks,
        near_blocks,
        near_leaf.T,
        near_count.reshape(1, 32),
        far_slots.T,
        far_count.reshape(1, 32),
        recv_rows.reshape(1, 128),
        coarse_blocks,
        coarse_far,
        coarse_count.reshape(1, 4),
    )


def solution(mesh):
    in_specs = (
        P("grp", "leaf"),
        P(None, "leaf"),
        P("leaf", None),
        P("leaf", None, None),
        P("leaf", None, None),
        P("leaf", None),
        P("leaf"),
        P("leaf", None),
        P("leaf"),
        P("leaf", None, None),
        P("leaf", "grp", None),
        P("leaf", None),
        P("leaf"),
    )
    out_specs = P("grp", "leaf")
    return jax.shard_map(
        per_device, mesh=mesh, in_specs=in_specs, out_specs=out_specs, check_vma=False
    )
```
